32 devices in a mesh: dp: 8 (over z, x), tensor: 4 (over y, core).
Axes of the slice: x: 2, y: 2, z: 4, core: 2. Of those that a mesh axis runs over, the one named last changes fastest.
Arguments:
- tokens: bfloat16 [8, 1024, 1024], P('dp', 'tensor'), may hold values from -6 to 6
- clip_counts: int32 [8], P('dp'), may hold values from 0 to 1, as said below
- cotangent: bfloat16 [8, 1024, 1024], P('dp', 'tensor'), may hold values from -6 to 6
- norm1_gain: bfloat16 [2, 1024], P(None, 'dp'), may hold values from 0.5 to 1.5
- norm1_shift: bfloat16 [2, 1024], P(None, 'dp'), may hold values from -1.25 to 1.25
- w_query: bfloat16 [2, 1024, 1024], P(None, 'dp', 'tensor'), may hold values from -0.1875 to 0.1875
- query_bias: bfloat16 [2, 1024], P(None, 'dp'), may hold values from -3 to 3
- w_key: bfloat16 [2, 1024, 1024], P(None, 'dp', 'tensor'), may hold values from -0.1875 to 0.1875
- w_value: bfloat16 [2, 1024, 1024], P(None, 'dp', 'tensor'), may hold values from -0.1875 to 0.1875
- value_bias: bfloat16 [2, 1024], P(None, 'dp'), may hold values from -3 to 3
- w_out: bfloat16 [2, 1024, 1024], P(None, 'dp', 'tensor'), may hold values from -3 to 3
- out_bias: bfloat16 [2, 1024], P(None, 'dp'), may hold values from -1.75 to 1.75
- norm2_gain: bfloat16 [2, 1024], P(None, 'dp'), may hold values from 0.5 to 1.5
- norm2_shift: bfloat16 [2, 1024], P(None, 'dp'), may hold values from -1.25 to 1.25
- w_up: bfloat16 [2, 1024, 4096], P(None, 'dp', 'tensor'), may hold values from -0.1875 to 0.1875
- up_bias: bfloat16 [2, 4096], P(None, 'dp'), may hold values from -3 to 3
- w_down: bfloat16 [2, 1024, 4096], P(None, 'dp', 'tensor'), may hold values from -0.09375 to 0.09375
- down_bias: bfloat16 [2, 1024], P(None, 'dp'), may hold values from -1.75 to 1.75
Outputs:
- mixed: bfloat16 [8, 1024, 1024], P('dp', 'tensor')
- tokens_grad: float32 [8, 1024, 1024], P('dp', 'tensor')
- grad_norm1_gain: float32 [2, 1024], P(None, 'dp')
- grad_norm1_shift: float32 [2, 1024], P(None, 'dp')
- grad_w_query: float32 [2, 1024, 1024], P(None, 'dp', 'tensor')
- grad_query_bias: float32 [2, 1024], P(None, 'dp')
- grad_w_key: float32 [2, 1024, 1024], P(None, 'dp', 'tensor')
- grad_w_value: float32 [2, 1024, 1024], P(None, 'dp', 'tensor')
- grad_value_bias: float32 [2, 1024], P(None, 'dp')
- grad_w_out: float32 [2, 1024, 1024], P(None, 'dp', 'tensor')
- grad_out_bias: float32 [2, 1024], P(None, 'dp')
- grad_norm2_gain: float32 [2, 1024], P(None, 'dp')
- grad_norm2_shift: float32 [2, 1024], P(None, 'dp')
- grad_w_up: float32 [2, 1024, 4096], P(None, 'dp', 'tensor')
- grad_up_bias: float32 [2, 4096], P(None, 'dp')
- grad_w_down: float32 [2, 1024, 4096], P(None, 'dp', 'tensor')
- grad_down_bias: float32 [2, 1024], P(None, 'dp')
The draws below stay inside these ranges and needn't reach their ends.
Inputs may be any that keep to these rules, and one draw needn't show every extreme that they name: clip_counts holds each slot's number of clips; some slot holds one clip and some slot none in every draw.
All inputs are finite; a program needn't handle non-finite values.
Results may differ from the reference program's by a relative error of at most 0.017.
Values may be sent and summed in bfloat16 or wider, within the bound.
A program may use at most 192 MiB of HBM per device.

```python
import jax
import jax.numpy as jnp
from jax import lax

D = 1024
HEADS = 16
HD = 64
FF = 4096
LAYERS = 2
LEN = 1024
GROUPS = 8


def draw_clip_counts(key, part):
    key = jax.random.fold_in(key, 7)
    first_key, second_key, third_key = jax.random.split(key, 3)
    raw_draw = jax.random.randint(first_key, (GROUPS,), 0, 64)
    live_slots = (raw_draw < 41).astype(jnp.int32)
    first_slot = jax.random.randint(second_key, (), 0, GROUPS)
    second_slot = (first_slot + 1 + jax.random.randint(third_key, (), 0, GROUPS - 1)) % GROUPS
    return live_slots.at[first_slot].set(1).at[second_slot].set(0)


def raised(array, stream_key, source, target, parts, factor):
    owner, partner = [(jnp.arange(array.shape[axis_at]) // (array.shape[axis_at] // parts)).reshape([-1 if axis == axis_at else 1 for axis in range(array.ndim)]) for axis_at in (source, target)]
    chosen = jax.random.permutation(stream_key, parts)[partner]
    strong = (owner == chosen) | (owner == (partner + parts // 2) % parts)
    return jnp.where(strong, factor * array, array)


def levels(own_key, shape, cuts, smallest, high):
    loudness = 1.0
    for position, parts in cuts:
        steps = jax.random.uniform(jax.random.fold_in(jax.random.fold_in(own_key, 6), position), (parts,), jnp.float32, smallest / len(cuts), high / len(cuts))
        loudness = loudness * jnp.repeat(jnp.exp(steps), shape[position] // parts).reshape((-1,) + (1,) * (len(shape) - 1 - position))
    return loudness


def normal_values(stream_key, dims, width, bound, pieces=(), dtype=jnp.bfloat16):
    gain = levels(stream_key, dims, pieces, -0.22, 0.18) if pieces else 1.0
    entries = jax.random.normal(stream_key, dims, jnp.float32) * width * gain
    return jnp.minimum(jnp.maximum(entries, -bound), bound).astype(dtype)


def bell_draw_with(rng, dims, width, limit, cuts, heavy, dtype=jnp.bfloat16):
    array = width * jax.random.normal(rng, dims, jnp.float32)
    if cuts:
        array = array * levels(rng, dims, cuts, -0.22, 0.18)
    return jnp.clip(raised(array, jax.random.fold_in(rng, 3), *heavy), -limit, limit).astype(dtype)


def setup_inputs(seed: int = 0) -> dict:
    arg_keys = jax.random.split(jax.random.key(seed), 19)
    return {
        "tokens": normal_values(arg_keys[0], (GROUPS, LEN, D), 1.0, 6.0, ((0, 8), (1, 4))),
        "clip_counts": draw_clip_counts(jax.random.fold_in(arg_keys[18], 71), 0),
        "cotangent": bell_draw_with(arg_keys[2], (GROUPS, LEN, D), 1.0, 6.0, ((0, 8), (1, 4)), (0, 2, 8, 2.0)),
        "norm1_gain": jnp.clip(1.0 + 0.1 * jax.random.normal(arg_keys[3], (LAYERS, D), jnp.float32), 0.5, 1.5).astype(jnp.bfloat16),
        "norm1_shift": normal_values(arg_keys[4], (LAYERS, D), 0.2, 1.25, ((1, 8),)),
        "w_query": normal_values(arg_keys[5], (LAYERS, D, D), D ** -0.5, 0.1875, ((1, 8), (2, 4))),
        "query_bias": normal_values(arg_keys[6], (LAYERS, D), 0.5, 3.0, ((1, 8),)),
        "w_key": normal_values(arg_keys[7], (LAYERS, D, D), D ** -0.5, 0.1875, ((1, 8), (2, 4))),
        "w_value": normal_values(arg_keys[8], (LAYERS, D, D), D ** -0.5, 0.1875, ((1, 8), (2, 4))),
        "value_bias": normal_values(arg_keys[9], (LAYERS, D), 0.5, 3.0, ((1, 8),)),
        "w_out": normal_values(arg_keys[10], (LAYERS, D, D), (max(4, D // 256)) ** -0.5, 3.0, ((1, 8), (2, 4))),
        "out_bias": normal_values(arg_keys[11], (LAYERS, D), 0.3, 1.75, ((1, 8),)),
        "norm2_gain": jnp.clip(1.0 + 0.1 * jax.random.normal(arg_keys[12], (LAYERS, D), jnp.float32), 0.5, 1.5).astype(jnp.bfloat16),
        "norm2_shift": normal_values(arg_keys[13], (LAYERS, D), 0.2, 1.25, ((1, 8),)),
        "w_up": normal_values(arg_keys[14], (LAYERS, D, FF), D ** -0.5, 0.1875, ((1, 8), (2, 4))),
        "up_bias": normal_values(arg_keys[15], (LAYERS, FF), 0.5, 3.0, ((1, 8),)),
        "w_down": normal_values(arg_keys[16], (LAYERS, D, FF), FF ** -0.5, 0.09375, ((1, 8), (2, 4))),
        "down_bias": normal_values(arg_keys[17], (LAYERS, D), 0.3, 1.75, ((1, 8),)),
    }


highest = lax.Precision.HIGHEST
norm_eps = 1e-06

@jax.custom_vjp
def low(v):
    return lax.optimization_barrier(v.astype(jnp.bfloat16)).astype(jnp.float32)

@jax.custom_vjp
def low_back(v):
    return v

def low_keep(v):
    return (low(v), None)

def low_pass(kept, grad):
    return (grad,)

def back_keep(v):
    return (v, None)

def back_low(kept, grad):
    return (low(grad),)
low.defvjp(low_keep, low_pass)
low_back.defvjp(back_keep, back_low)

def layer_norm(inputs, gain_vec, shift_vec):
    row_mean = lax.optimization_barrier(jnp.mean(inputs, axis=-1, keepdims=True))
    centered = inputs - row_mean
    variance = lax.optimization_barrier(jnp.mean(centered * centered, axis=-1, keepdims=True))
    return centered * lax.rsqrt(variance + norm_eps) * gain_vec + shift_vec

def linear(inputs, weight_mat):
    return jnp.dot(inputs, weight_mat, precision=highest)

def attention(queries, key_rows, value_rows):
    seq_len = queries.shape[0]
    block_count = max(1, seq_len // 512)
    block_rows = seq_len // block_count
    key_heads = key_rows.reshape(seq_len, HEADS, HD)
    value_heads = value_rows.reshape(seq_len, HEADS, HD)

    def one_block(query_block):
        scores = low_back(jnp.einsum('qhd,khd->hqk', query_block, key_heads, precision=highest) * HD ** (-0.5))
        prob_rows = low(jax.nn.softmax(scores, axis=-1))
        return jnp.einsum('hqk,khd->qhd', prob_rows, value_heads, precision=highest)
    outputs = lax.map(jax.checkpoint(one_block), queries.reshape(block_count, block_rows, HEADS, HD))
    return outputs.reshape(seq_len, HEADS * HD)

def encoder_layer(hidden_rows, params):
    gain_first, shift_first, query_mat, query_offset, key_mat, value_mat, value_offset, out_mat, out_offset, gain_second, shift_second, up_mat, up_offset, down_mat, down_offset = params
    normed = low(layer_norm(hidden_rows, gain_first, shift_first))
    queries = low_back(low(linear(normed, query_mat) + query_offset))
    key_rows = low_back(low(linear(normed, key_mat)))
    value_rows = low_back(low(linear(normed, value_mat) + value_offset))
    attended = low_back(low(attention(queries, key_rows, value_rows)))
    middle = hidden_rows + low_back(linear(attended, out_mat.T) + out_offset)
    normed_two = low(layer_norm(middle, gain_second, shift_second))
    pre_act = low_back(linear(normed_two, up_mat) + up_offset)
    activated = low(jax.nn.gelu(pre_act, approximate=False))
    return middle + low_back(linear(activated, down_mat.T) + down_offset)

def reference(tokens, clip_counts, cotangent, norm1_gain, norm1_shift, w_query, query_bias, w_key, w_value, value_bias, w_out, out_bias, norm2_gain, norm2_shift, w_up, up_bias, w_down, down_bias):
    params = tuple((member.astype(jnp.float32) for member in (norm1_gain, norm1_shift, w_query, query_bias, w_key, w_value, value_bias, w_out, out_bias, norm2_gain, norm2_shift, w_up, up_bias, w_down, down_bias)))
    live_mask = clip_counts.astype(jnp.float32)

    def forward(hidden_rows, weights):
        for layer_index in range(LAYERS):
            hidden_rows = encoder_layer(hidden_rows, [member[layer_index] for member in weights])
        return hidden_rows

    def per_clip(totals, inputs):
        clip_rows, cot_rows, live_one = inputs
        result, pullback = jax.vjp(forward, clip_rows.astype(jnp.float32), params)
        rows_grad, param_grads = pullback(cot_rows.astype(jnp.float32) * live_one)
        totals = jax.tree.map(jnp.add, totals, param_grads)
        return (totals, (result.astype(jnp.bfloat16), rows_grad))
    starting = jax.tree.map(jnp.zeros_like, params)
    totals, (mixed, tokens_grad) = lax.scan(per_clip, starting, (tokens, cotangent, live_mask))
    return (mixed, tokens_grad, totals[0], totals[1], totals[2], totals[3], totals[4], totals[5], totals[6], totals[7], totals[8], totals[9], totals[10], totals[11], totals[12], totals[13], totals[14])
```

```python
import functools
import math

import jax
import jax.numpy as jnp
from jax import lax
from jax.experimental import pallas as pl
from jax.experimental.pallas import tpu as pltpu
from jax.sharding import PartitionSpec as P

HD = 64
norm_eps = 1e-06
MESH = pl.DeviceIdType.MESH
bf16 = jnp.bfloat16
f32 = jnp.float32
ROOT_HALF = 1.0 / math.sqrt(2.0)
PHI_ZERO = 1.0 / math.sqrt(2.0 * math.pi)
LOG2E = 1.0 / math.log(2.0)
CHUNK = 64


def dot_nn(left, right):
    return jnp.dot(left, right, preferred_element_type=f32)


def dot_nt(left, right):
    return lax.dot_general(left, right, (((1,), (1,)), ((), ())), preferred_element_type=f32)


def dot_tn(left, right):
    return lax.dot_general(left, right, (((0,), (0,)), ((), ())), preferred_element_type=f32)


def repeat(low, high, body):
    if high - low <= 4:
        for index in range(low, high):
            body(index)
    else:

        @pl.loop(low, high)
        def _(index):
            body(index)


def norm_parts(rows):
    centered = rows - jnp.mean(rows, axis=-1, keepdims=True)
    scale = lax.rsqrt(jnp.mean(centered * centered, axis=-1, keepdims=True) + norm_eps)
    return centered * scale, scale


def encoder_kernel(
    dims,
    tok, cot, counts, wq, wk, wv, wo, wu, wd, vec,
    mixed, tgrad, gq, gk, gv, go, gu, gd, vg, spill,
    W, NF, QKV, AT, LSE, X, MID, NF2, ACT, GP, GF, MF, DQKV, DO, GC, BR, AR,
    SA, SB, SC, RA, RB, RC, ACC, OST, VT, KT, DKA, DVA, STB,
    loc, ag_s, ag_r, rs_s, rs_r, wz_s, wz_r, wx_s, wx_r, gb_s, gb_r, ga_s, ga_r, cred_b, cred_a,
):
    A, B, S, R, D, HC, FC = dims
    heads = HC // HD
    score_scale = HD ** (-0.5)
    dp = lax.axis_index("dp")
    t = lax.axis_index("tensor")
    a = dp // B
    b = dp % B
    y = t // 2
    c = t % 2

    def flip(i):
        return 2 * ((y + i // 2) % 2) + (c + i % 2) % 2

    sib = (dp, flip(1))
    ypeer = (dp, flip(2))

    def dp_dev(aa, bb):
        return (aa * B + bb, t)

    def far(k):
        return (a + k) % A

    def near(j):
        return (b + j) % B

    groups = ((0, 3 * HC), (3 * HC, HC), (4 * HC, FC), (4 * HC + FC, FC))

    def blk(i):
        return pl.ds(pl.multiple_of(i * R, R), R)

    def shard(aa, bb):
        return pl.ds(pl.multiple_of((aa * B + bb) * S, S), S)

    def remote(src, dst, send, recv, device):
        return pltpu.make_async_remote_copy(
            src_ref=src, dst_ref=dst, send_sem=send, recv_sem=recv, device_id=device, device_id_type=MESH
        )

    barrier = pltpu.get_barrier_semaphore()

    def greet(device):
        pl.semaphore_signal(barrier, inc=1, device_id=device, device_id_type=MESH)

    greet(sib)
    greet(ypeer)
    repeat(1, A, lambda k: greet(dp_dev(far(k), b)))
    repeat(1, B, lambda j: greet(dp_dev(a, near(j))))

    def load_weight(l, g):
        parts = {
            0: ((wq, 0, HC), (wk, HC, HC), (wv, 2 * HC, HC)),
            1: ((wo, 3 * HC, HC),),
            2: ((wu, 4 * HC, FC),),
            3: ((wd, 4 * HC + FC, FC),),
        }[g]
        return [
            pltpu.make_async_copy(
                src.at[l], W.at[l, shard(a, b), pl.ds(first, width)], loc.at[l, 2 * g + place if g == 0 else g + 2]
            )
            for place, (src, first, width) in enumerate(parts)
        ]

    for l in range(2):
        for g in range(4):
            for copy in load_weight(l, g):
                copy.start()
    tok_copy = pltpu.make_async_copy(tok.at[0], STB, loc.at[0, 6])
    tok_copy.start()
    pl.semaphore_wait(barrier, A + B)

    def wrow(l, aa, bb, g):
        return W.at[l, shard(aa, bb), pl.ds(groups[g][0], groups[g][1])]

    def wz(l, g, k, source, device):
        ref = wrow(l, source, b, g)
        return remote(ref, ref, wz_s.at[l, g, k], wz_r.at[l, g, k], device)

    def wx(l, g, k, j, minor, device):
        ref = wrow(l, (a - k + A) % A, minor, g)
        return remote(ref, ref, wx_s.at[l, g, k, j], wx_r.at[l, g, k, j], device)

    def w_send_x(l, g, k):
        repeat(1, B, lambda j: wx(l, g, k, j, b, dp_dev(a, near(j))).start())

    def w_start(l, g):
        for copy in load_weight(l, g):
            copy.wait()
        repeat(1, A, lambda k: wz(l, g, k, a, dp_dev(far(k), b)).start())
        w_send_x(l, g, 0)

    def w_pump(l, g):
        def one(k):
            wz(l, g, k, (a - k + A) % A, dp_dev(far(k), b)).wait_recv()
            w_send_x(l, g, k)

        repeat(1, A, one)

    def w_done(l, g):
        def one(k):
            repeat(1, B, lambda j: wx(l, g, k, j, (b - j + B) % B, dp_dev(a, near(j))).wait_recv())

        repeat(0, A, one)

    def w_sent(l, g):
        repeat(1, A, lambda k: wz(l, g, k, a, dp_dev(far(k), b)).wait_send())

        def one(k):
            repeat(1, B, lambda j: wx(l, g, k, j, b, dp_dev(a, near(j))).wait_send())

        repeat(0, A, one)

    def ag_copy(buf, kind):
        row = blk(t) if kind < 2 else blk(flip(2))
        return remote(buf.at[row], buf.at[row], ag_s.at[kind], ag_r.at[kind], ypeer if kind == 0 else sib)

    def ag_start(buf):
        ag_copy(buf, 0).start()
        ag_copy(buf, 1).start()

    def ag_wait(buf, i):
        @pl.when(i == 1)
        def _():
            ref = buf.at[blk(flip(1))]
            remote(ref, ref, ag_s.at[1], ag_r.at[1], sib).wait_recv()

        @pl.when(i == 2)
        def _():
            ref = buf.at[blk(flip(2))]
            remote(ref, ref, ag_s.at[0], ag_r.at[0], ypeer).wait_recv()
            ag_copy(buf, 2).start()

        @pl.when(i == 3)
        def _():
            ref = buf.at[blk(flip(3))]
            remote(ref, ref, ag_s.at[2], ag_r.at[2], sib).wait_recv()
            for kind in range(3):
                ag_copy(buf, kind).wait_send()

    rs_a = remote(SA, RA, rs_s.at[0], rs_r.at[0], sib)
    rs_b = remote(SB, RB, rs_s.at[1], rs_r.at[1], ypeer)
    rs_c = remote(SC, RC, rs_s.at[2], rs_r.at[2], sib)

    def rs_run(part):
        @pl.loop(0, 4)
        def _(step):
            ACC[...] = part(flip(3 - step))

            @pl.when(step == 0)
            def _():
                SA[...] = ACC[...].astype(bf16)
                rs_a.start()

            @pl.when(step == 1)
            def _():
                rs_a.wait_recv()
                SB[...] = (ACC[...] + RA[...].astype(f32)).astype(bf16)
                rs_b.start()

            @pl.when(step == 2)
            def _():
                SC[...] = ACC[...].astype(bf16)
                rs_c.start()

    def rs_wait():
        rs_c.wait_recv()
        rs_b.wait_recv()

    def rs_sum(row):
        return ACC[row, :] + RB[row, :].astype(f32) + RC[row, :].astype(f32)

    def rs_end():
        rs_a.wait_send()
        rs_b.wait_send()
        rs_c.wait_send()

    def by_chunk(body):
        @pl.loop(0, R // CHUNK)
        def _(index):
            body(pl.ds(pl.multiple_of(index * CHUNK, CHUNK), CHUNK), pl.ds(pl.multiple_of(t * R + index * CHUNK, CHUNK), CHUNK))

    def head_mask(h):
        lane = lax.broadcasted_iota(jnp.int32, (R, HC), 1)
        return (lane >= h * HD) & (lane < (h + 1) * HD)

    order = [(l, g) for l in range(2) for g in range(4)]
    w_start(*order[0])
    w_start(*order[1])
    tok_copy.wait()

    def load_tokens(row, full):
        X[0, row, :] = STB[row, :].astype(f32)

    by_chunk(load_tokens)

    def pump(index):
        w_pump(*order[index])
        if index + 2 < len(order):
            w_start(*order[index + 2])

    spills = [
        pltpu.make_async_copy(
            W.at[0, :, pl.ds(first, width)], spill.at[:, pl.ds(first, width)], loc.at[1, 6 + g]
        )
        for g, (first, width) in enumerate(groups)
    ]

    for l in range(2):

        def first_norm(row, full):
            n, _ = norm_parts(X[l, row, :])
            NF[l, full, :] = (n * vec[l, 0:1, :] + vec[l, 1:2, :]).astype(bf16)

        by_chunk(first_norm)
        ag_start(NF.at[l])
        pump(4 * l)
        w_done(l, 0)

        @pl.loop(0, 4)
        def _(i):
            ag_wait(NF.at[l], i)
            row = blk(flip(i))
            out = dot_nn(NF[l, row, :], W[l, :, 0 : 3 * HC])
            QKV[l, row, 0:HC] = (out[:, 0:HC] + vec[l, 7:8, 0:HC]).astype(bf16)
            QKV[l, row, HC : 2 * HC] = out[:, HC : 2 * HC].astype(bf16)
            QKV[l, row, 2 * HC : 3 * HC] = (out[:, 2 * HC : 3 * HC] + vec[l, 7:8, HC : 2 * HC]).astype(bf16)

        VT[...] = QKV[l, :, 2 * HC : 3 * HC].T
        pump(4 * l + 1)
        w_done(l, 1)

        def attend(i):
            row = blk(i)
            queries = QKV[l, row, 0:HC]
            keys = QKV[l, :, HC : 2 * HC]
            outs = []
            for h in range(heads):
                masked = jnp.where(head_mask(h), queries, jnp.zeros_like(queries))
                scores = dot_nt(keys, masked) * (score_scale * LOG2E)
                top = jnp.max(scores, axis=0, keepdims=True)
                exps = jnp.exp2(scores - top)
                total = jnp.sum(exps, axis=0, keepdims=True)
                LSE[l, h : h + 1, row] = top + jnp.log(total) * LOG2E
                outs.append(dot_nn(VT[h * HD : (h + 1) * HD, :], exps.astype(bf16)) * (1.0 / total))
            AT[l, row, :] = jnp.concatenate(outs, axis=0).T.astype(bf16)
            return dot_nt(AT[l, row, :], W[l, :, 3 * HC : 4 * HC])

        rs_run(attend)
        rs_wait()

        def second_norm(row, full):
            middle = X[l, row, :] + rs_sum(row) + vec[l, 2:3, :]
            MID[l, row, :] = middle
            n, _ = norm_parts(middle)
            NF2[l, full, :] = (n * vec[l, 3:4, :] + vec[l, 4:5, :]).astype(bf16)

        by_chunk(second_norm)
        rs_end()
        ag_start(NF2.at[l])
        pump(4 * l + 2)
        w_done(l, 2)

        @pl.loop(0, 4)
        def _(i):
            ag_wait(NF2.at[l], i)
            row = blk(flip(i))
            pre = dot_nn(NF2[l, row, :], W[l, :, 4 * HC : 4 * HC + FC]) + vec[l, 6:7, :]
            cumul = 0.5 * (1.0 + lax.erf(pre * ROOT_HALF))
            ACT[l, row, :] = (pre * cumul).astype(bf16)
            GP[l, row, :] = (cumul + pre * (jnp.exp(-0.5 * pre * pre) * PHI_ZERO)).astype(bf16)

        pump(4 * l + 3)
        w_done(l, 3)
        rs_run(lambda i: dot_nt(ACT[l, blk(i), :], W[l, :, 4 * HC + FC : 4 * HC + 2 * FC]))
        if l == 0:
            for g in range(4):
                w_sent(0, g)
            for copy in spills:
                copy.start()
        rs_wait()

        def layer_out(row, full):
            out = MID[l, row, :] + rs_sum(row) + vec[l, 5:6, :]
            if l == 0:
                X[1, row, :] = out
            else:
                STB[row, :] = out.astype(bf16)

        by_chunk(layer_out)
        rs_end()

    mixed_copy = pltpu.make_async_copy(STB, mixed.at[0], loc.at[0, 6])
    mixed_copy.start()
    for g in range(4):
        w_sent(1, g)
    for copy in spills:
        copy.wait()
    mixed_copy.wait()
    cot_copy = pltpu.make_async_copy(cot.at[0], STB, loc.at[0, 7])
    cot_copy.start()
    cot_copy.wait()
    live = counts[0].astype(f32)

    def load_cot(row, full):
        GC[row, :] = STB[row, :].astype(f32) * live

    by_chunk(load_cot)
    vg[...] = jnp.zeros_like(vg)

    def gsrc(l, g):
        first, width = groups[g]
        if l == 1:
            return W, 0, first, width
        if g == 3:
            return ACT, 1, 0, width
        if g == 2:
            return GP, 1, 0, width
        return NF2, 1, (0 if g == 0 else 3 * HC), width

    def gref(l, g, aa, bb):
        buf, slot, first, width = gsrc(l, g)
        return buf.at[slot, shard(aa, bb), pl.ds(first, width)]

    def gb(l, g, j, aa):
        first, width = groups[g]
        return remote(
            gref(l, g, aa, near(j)), BR.at[j - 1, aa, :, pl.ds(first, width)], gb_s.at[l, g, j, aa], gb_r.at[l, g, j, aa],
            dp_dev(a, near(j)),
        )

    def ga(l, g, k):
        first, width = groups[g]
        return remote(
            gref(l, g, far(k), b), AR.at[k - 1, :, pl.ds(first, width)], ga_s.at[l, g, k], ga_r.at[l, g, k], dp_dev(far(k), b)
        )

    def g_start(l, g):
        if l == 0:
            pl.semaphore_wait(cred_b.at[g], B - 1)

        def one(k):
            repeat(1, B, lambda j: gb(l, g, j, far(k)).start())

        repeat(1, A + 1, one)

    def g_piece(l, g, aa):
        first, width = groups[g]
        repeat(1, B, lambda j: gb(l, g, j, aa).wait_recv())
        total = gref(l, g, aa, b)[...].astype(f32)
        for j in range(1, B):
            total = total + BR[j - 1, aa, :, first : first + width].astype(f32)
        return total

    def g_pump(l, g):
        first, width = groups[g]
        if l == 0:
            pl.semaphore_wait(cred_a.at[g], A - 1)

        def one(k):
            piece = gref(l, g, far(k), b)
            piece[...] = g_piece(l, g, far(k)).astype(bf16)
            ga(l, g, k).start()

        repeat(1, A, one)
        OST[l, :, first : first + width] = g_piece(l, g, a)
        if l == 1:
            repeat(
                1, B,
                lambda j: pl.semaphore_signal(cred_b.at[g], inc=1, device_id=dp_dev(a, near(j)), device_id_type=MESH),
            )

    def g_out(l, g):
        parts = {0: ((gq, 0, HC), (gk, HC, HC), (gv, 2 * HC, HC)), 1: ((go, 0, HC),), 2: ((gu, 0, FC),), 3: ((gd, 0, FC),)}[g]
        first = groups[g][0]
        return [
            pltpu.make_async_copy(
                OST.at[l, :, pl.ds(first + at, width)], dst.at[l], loc.at[l, 2 * g + place if g == 0 else g + 2]
            )
            for place, (dst, at, width) in enumerate(parts)
        ]

    def g_final(l, g):
        first, width = groups[g]

        def one(k):
            ga(l, g, k).wait_recv()
            OST[l, :, first : first + width] += AR[k - 1, :, first : first + width].astype(f32)

        repeat(1, A, one)
        if l == 1:
            repeat(
                1, A,
                lambda k: pl.semaphore_signal(cred_a.at[g], inc=1, device_id=dp_dev(far(k), b), device_id_type=MESH),
            )
        for copy in g_out(l, g):
            copy.start()

    def g_sent(l, g):
        repeat(1, A, lambda k: ga(l, g, k).wait_send())

        def one(k):
            repeat(1, B, lambda j: gb(l, g, j, far(k)).wait_send())

        repeat(1, A + 1, one)
        for copy in g_out(l, g):
            copy.wait()

    def weight_grad(l, g, left, right):
        buf, slot, first, width = gsrc(l, g)

        @pl.loop(0, D // R)
        def _(i):
            buf[slot, blk(i), first : first + width] = dot_tn(left[:, blk(i)], right[...]).astype(bf16)

        g_start(l, g)

    def reload(g):
        first, width = groups[g]
        return pltpu.make_async_copy(spill.at[:, pl.ds(first, width)], W.at[1, :, pl.ds(first, width)], loc.at[1, 6 + g])

    for l in (1, 0):

        def low_grad(row, full):
            low = GC[row, :].astype(bf16)
            GF[full, :] = low
            vg[l, 5:6, :] += jnp.sum(low.astype(f32), axis=0, keepdims=True)

        by_chunk(low_grad)
        ag_start(GF)
        if l == 0:
            reload(3).wait()
            reload(2).wait()
            g_pump(1, 1)

        @pl.loop(0, 4)
        def _(i):
            ag_wait(GF, i)
            row = blk(flip(i))
            act_grad = dot_nn(GF[row, :], W[1, :, 4 * HC + FC : 4 * HC + 2 * FC])
            pre_grad = (act_grad * GP[l, row, :].astype(f32)).astype(bf16)
            GP[l, row, :] = pre_grad
            vg[l, 6:7, :] += jnp.sum(pre_grad.astype(f32), axis=0, keepdims=True)

        rs_run(lambda i: dot_nt(GP[l, blk(i), :], W[1, :, 4 * HC : 4 * HC + FC]))
        if l == 1:
            reload(2).start()
            reload(3).start()
        if l == 0:
            g_pump(1, 0)
        weight_grad(l, 3, GF, ACT.at[l])
        weight_grad(l, 2, NF2.at[l], GP.at[l])
        rs_wait()

        def second_back(row, full):
            dy = rs_sum(row)
            n, scale = norm_parts(MID[l, row, :])
            vg[l, 3:4, :] += jnp.sum(dy * n, axis=0, keepdims=True)
            vg[l, 4:5, :] += jnp.sum(dy, axis=0, keepdims=True)
            dn = dy * vec[l, 3:4, :]
            part = scale * (
                dn - jnp.mean(dn, axis=-1, keepdims=True) - n * jnp.mean(dn * n, axis=-1, keepdims=True)
            )
            grad = GC[row, :] + part
            GC[row, :] = grad
            low = grad.astype(bf16)
            MF[full, :] = low
            vg[l, 2:3, :] += jnp.sum(low.astype(f32), axis=0, keepdims=True)

        by_chunk(second_back)
        rs_end()
        ag_start(MF)
        if l == 0:
            reload(1).wait()
            reload(0).wait()

        @pl.loop(0, 4)
        def _(i):
            ag_wait(MF, i)
            row = blk(flip(i))
            DO[row, :] = dot_nn(MF[row, :], W[1, :, 3 * HC : 4 * HC]).astype(bf16)

        weight_grad(l, 1, MF, AT.at[l])
        if l == 0:
            g_final(1, 1)
            g_final(1, 0)
        g_pump(l, 3)
        if l == 1:
            reload(1).start()
        KT[...] = QKV[l, :, HC : 2 * HC].T
        DKA[...] = jnp.zeros_like(DKA)
        DVA[...] = jnp.zeros_like(DVA)

        @pl.loop(0, 4)
        def _(i):
            row = blk(i)
            queries = QKV[l, row, 0:HC]
            keys = QKV[l, :, HC : 2 * HC]
            values = QKV[l, :, 2 * HC : 3 * HC]
            out_grads = DO[row, :]
            parts = []
            for h in range(heads):
                mask = head_mask(h)
                q_one = jnp.where(mask, queries, jnp.zeros_like(queries))
                do_one = jnp.where(mask, out_grads, jnp.zeros_like(out_grads))
                probs = jnp.exp2(dot_nt(keys, q_one) * (score_scale * LOG2E) - LSE[l, h : h + 1, row])
                prob_grad = dot_nt(values, do_one)
                DVA[...] += dot_nn(probs.astype(bf16), do_one)
                row_dot = jnp.sum(probs * prob_grad, axis=0, keepdims=True)
                score_grad = (probs * (prob_grad - row_dot)).astype(bf16)
                DKA[...] += dot_nn(score_grad, q_one)
                parts.append(dot_nn(KT[h * HD : (h + 1) * HD, :], score_grad))
            DQKV[row, 0:HC] = (jnp.concatenate(parts, axis=0).T * score_scale).astype(bf16)

        g_pump(l, 2)
        DQKV[:, HC : 2 * HC] = (DKA[...] * score_scale).astype(bf16)
        DQKV[:, 2 * HC : 3 * HC] = DVA[...].astype(bf16)
        rs_run(lambda i: dot_nt(DQKV[blk(i), :], W[1, :, 0 : 3 * HC]))
        if l == 1:
            reload(0).start()
        weight_grad(l, 0, NF.at[l], DQKV)
        vg[l, 7:8, 0:HC] = jnp.sum(DQKV[:, 0:HC].astype(f32), axis=0, keepdims=True)
        vg[l, 7:8, HC : 2 * HC] = jnp.sum(DQKV[:, 2 * HC : 3 * HC].astype(f32), axis=0, keepdims=True)
        g_final(l, 3)
        rs_wait()

        def first_back(row, full):
            dy = rs_sum(row)
            n, scale = norm_parts(X[l, row, :])
            vg[l, 0:1, :] += jnp.sum(dy * n, axis=0, keepdims=True)
            vg[l, 1:2, :] += jnp.sum(dy, axis=0, keepdims=True)
            dn = dy * vec[l, 0:1, :]
            part = scale * (
                dn - jnp.mean(dn, axis=-1, keepdims=True) - n * jnp.mean(dn * n, axis=-1, keepdims=True)
            )
            GC[row, :] = GC[row, :] + part

        by_chunk(first_back)
        rs_end()
        g_final(l, 2)

    grad_copy = pltpu.make_async_copy(GC, tgrad.at[0], loc.at[0, 7])
    grad_copy.start()
    g_pump(0, 1)
    g_pump(0, 0)
    g_final(0, 1)
    g_final(0, 0)
    grad_copy.wait()
    for l in range(2):
        for g in range(4):
            g_sent(l, g)


def shards(
    mesh_dp,
    tokens, clip_counts, cotangent, norm1_gain, norm1_shift, w_query, query_bias, w_key, w_value, value_bias, w_out,
    out_bias, norm2_gain, norm2_shift, w_up, up_bias, w_down, down_bias,
):
    t = lax.axis_index("tensor")
    dp = lax.axis_index("dp")
    layers, S, HC = w_query.shape
    FC = w_up.shape[2]
    _, R, D = tokens.shape
    B = 1
    while 4 * B * B <= mesh_dp:
        B *= 2
    A = mesh_dp // B
    packed = jnp.concatenate(
        [
            jnp.stack(
                [norm1_gain, norm1_shift, out_bias, norm2_gain, norm2_shift, down_bias, query_bias, value_bias], axis=1
            ),
            up_bias.reshape(layers, -1, S),
        ],
        axis=1,
    )
    gathered = lax.all_gather(packed, "dp", axis=0)
    wide = gathered[:, :, :8].transpose(1, 2, 0, 3).reshape(layers, 8, D).astype(f32)
    up_full = gathered[:, :, 8:].transpose(1, 0, 2, 3).reshape(layers, 1, -1).astype(f32)
    up_own = lax.dynamic_slice_in_dim(up_full, t * FC, FC, 2)
    heads_own = lax.dynamic_slice_in_dim(wide[:, 6:8], t * HC, HC, 2).reshape(layers, 1, 2 * HC)
    vec = jnp.concatenate([wide[:, :6], up_own, jnp.pad(heads_own, ((0, 0), (0, 0), (0, D - 2 * HC)))], axis=1)

    LEN = 4 * R
    COLS = 4 * HC + 2 * FC
    dims = (A, B, S, R, D, HC, FC)
    vm = pltpu.VMEM
    dma = pltpu.SemaphoreType.DMA
    any_spec = pl.BlockSpec(memory_space=pl.ANY)
    vmem_spec = pl.BlockSpec(memory_space=pltpu.VMEM)
    grad_small = jax.ShapeDtypeStruct((layers, S, HC), f32)
    grad_large = jax.ShapeDtypeStruct((layers, S, FC), f32)
    outs = pl.pallas_call(
        functools.partial(encoder_kernel, dims),
        out_shape=(
            jax.ShapeDtypeStruct((1, R, D), bf16),
            jax.ShapeDtypeStruct((1, R, D), f32),
            grad_small, grad_small, grad_small, grad_small, grad_large, grad_large,
            jax.ShapeDtypeStruct((layers, 8, D), f32),
            jax.ShapeDtypeStruct((D, COLS), bf16),
        ),
        in_specs=[any_spec, any_spec, pl.BlockSpec(memory_space=pltpu.SMEM)] + [any_spec] * 6 + [vmem_spec],
        out_specs=tuple([any_spec] * 8 + [vmem_spec, any_spec]),
        scratch_shapes=[
            vm((2, D, COLS), bf16),
            vm((2, LEN, D), bf16),
            vm((2, LEN, 3 * HC), bf16),
            vm((2, LEN, HC), bf16),
            vm((2, 8, LEN), f32),
            vm((2, R, D), f32),
            vm((2, R, D), f32),
            vm((2, LEN, D), bf16),
            vm((2, LEN, FC), bf16),
            vm((2, LEN, FC), bf16),
            vm((LEN, D), bf16),
            vm((LEN, D), bf16),
            vm((LEN, 3 * HC), bf16),
            vm((LEN, HC), bf16),
            vm((R, D), f32),
            vm((max(B - 1, 1), A, S, COLS), bf16),
            vm((max(A - 1, 1), S, COLS), bf16),
            vm((R, D), bf16), vm((R, D), bf16), vm((R, D), bf16),
            vm((R, D), bf16), vm((R, D), bf16), vm((R, D), bf16),
            vm((R, D), f32),
            vm((2, S, COLS), f32),
            vm((HC, LEN), bf16), vm((HC, LEN), bf16),
            vm((LEN, HC), f32), vm((LEN, HC), f32),
            vm((R, D), bf16),
            dma((2, 10)),
            dma((3,)), dma((3,)), dma((3,)), dma((3,)),
            dma((2, 4, A)), dma((2, 4, A)), dma((2, 4, A, B)), dma((2, 4, A, B)),
            dma((2, 4, B, A)), dma((2, 4, B, A)), dma((2, 4, A)), dma((2, 4, A)),
            pltpu.SemaphoreType.REGULAR((4,)), pltpu.SemaphoreType.REGULAR((4,)),
        ],
        compiler_params=pltpu.CompilerParams(
            collective_id=0, has_side_effects=True, vmem_limit_bytes=64 * 2**20 - 2**17
        ),
        name="encoder",
    )(tokens, cotangent, clip_counts, w_query, w_key, w_value, w_out, w_up, w_down, vec)
    mixed, tokens_grad, gq, gk, gv, go, gu, gd, vg, _ = outs

    def place(part, full):
        return lax.dynamic_update_slice_in_dim(jnp.zeros((layers, full), f32), part, t * part.shape[1], 1)

    whole = jnp.concatenate(
        [vg[:, :6].reshape(layers, -1), place(vg[:, 7, :HC], D), place(vg[:, 7, HC : 2 * HC], D), place(vg[:, 6], 4 * FC)],
        axis=1,
    )
    whole = lax.psum(whole, ("dp", "tensor"))

    def own(index):
        return lax.dynamic_slice_in_dim(whole[:, index * D : (index + 1) * D], dp * S, S, 1)

    ub = lax.dynamic_slice_in_dim(whole[:, 8 * D :], dp * (4 * FC // mesh_dp), 4 * FC // mesh_dp, 1)
    return (
        mixed, tokens_grad, own(0), own(1), gq, own(6), gk, gv, own(7), go, own(2), own(3), own(4), gu, ub, gd, own(5),
    )


def solution(mesh):
    rows = P("dp", "tensor", None)
    vector = P(None, "dp")
    matrix = P(None, "dp", "tensor")
    return jax.shard_map(
        functools.partial(shards, mesh.shape["dp"]),
        mesh=mesh,
        in_specs=(
            rows, P("dp"), rows, vector, vector, matrix, vector, matrix, matrix, vector, matrix, vector, vector, vector,
            matrix, vector, matrix, vector,
        ),
        out_specs=(
            rows, rows, vector, vector, matrix, vector, matrix, matrix, vector, matrix, vector, vector, vector, matrix,
            vector, matrix, vector,
        ),
        check_vma=False,
    )
```

```python
import functools
import math

import jax
import jax.numpy as jnp
from jax import lax
from jax.experimental import pallas as pl
from jax.experimental.pallas import tpu as pltpu
from jax.sharding import PartitionSpec as P

HD = 64
norm_eps = 1e-06
MESH = pl.DeviceIdType.MESH
bf16 = jnp.bfloat16
f32 = jnp.float32
ROOT_HALF = 1.0 / math.sqrt(2.0)
PHI_ZERO = 1.0 / math.sqrt(2.0 * math.pi)
LOG2E = 1.0 / math.log(2.0)
CHUNK = 64


def dot_nn(left, right):
    return jnp.dot(left, right, preferred_element_type=f32)


def dot_nt(left, right):
    return lax.dot_general(left, right, (((1,), (1,)), ((), ())), preferred_element_type=f32)


def dot_tn(left, right):
    return lax.dot_general(left, right, (((0,), (0,)), ((), ())), preferred_element_type=f32)


def repeat(low, high, body):
    if high - low <= 4:
        for index in range(low, high):
            body(index)
    else:

        pl.loop(low, high)(body)


def norm_parts(rows):
    centered = rows - jnp.mean(rows, axis=-1, keepdims=True)
    scale = lax.rsqrt(jnp.mean(centered * centered, axis=-1, keepdims=True) + norm_eps)
    return centered * scale, scale


def encoder_kernel(
    dims,
    tok, cot, counts, wq, wk, wv, wo, wu, wd, gain_one, shift_one, out_b, gain_two, shift_two, down_b, query_b, value_b, up_b,
    mixed, tgrad, gq, gk, gv, go, gu, gd, vs_out, spill,
    W, NF, QKV, AT, LSE, X, MID, NF2, ACT, GP, GF, MF, DQKV, DO, GC, BR, AR,
    SA, SB, SC, RA, RB, RC, ACC, OST, VT, KT, DKA, DVA, STB, RAW, vec, vg, VGX, VGS, VGZ, VGU, VGT, VS, TOT,
    loc, ag_s, ag_r, rs_s, rs_r, wz_s, wz_r, wx_s, wx_r, gb_s, gb_r, ga_s, ga_r,
    vz_s, vz_r, vx_s, vx_r, vgx_s, vgx_r, vgz_s, vgz_r, vgt_s, vgt_r, cred_b, cred_a,
):
    A, B, S, R, D, HC, FC = dims
    heads = HC // HD
    score_scale = HD ** (-0.5)
    dp = lax.axis_index("dp")
    t = lax.axis_index("tensor")
    a = dp // B
    b = dp % B
    y = t // 2
    c = t % 2

    def flip(i):
        return 2 * ((y + i // 2) % 2) + (c + i % 2) % 2

    sib = (dp, flip(1))
    ypeer = (dp, flip(2))
    corner = (dp, flip(3))

    def dp_dev(aa, bb):
        return (aa * B + bb, t)

    def far(k):
        return (a + k) % A

    def near(j):
        return (b + j) % B

    groups = ((0, 3 * HC), (3 * HC, HC), (4 * HC, FC), (4 * HC + FC, FC))

    def blk(i):
        return pl.ds(pl.multiple_of(i * R, R), R)

    def shard(aa, bb):
        return pl.ds(pl.multiple_of((aa * B + bb) * S, S), S)

    def remote(src, dst, send, recv, device):
        return pltpu.make_async_remote_copy(
            src_ref=src, dst_ref=dst, send_sem=send, recv_sem=recv, device_id=device, device_id_type=MESH
        )

    barrier = pltpu.get_barrier_semaphore()

    def greet(device):
        pl.semaphore_signal(barrier, inc=1, device_id=device, device_id_type=MESH)

    greet(sib)
    greet(ypeer)
    greet(corner)
    repeat(1, A, lambda k: greet(dp_dev(far(k), b)))
    repeat(1, B, lambda j: greet(dp_dev(a, near(j))))

    def load_weight(l, g):
        parts = {
            0: ((wq, 0, HC), (wk, HC, HC), (wv, 2 * HC, HC)),
            1: ((wo, 3 * HC, HC),),
            2: ((wu, 4 * HC, FC),),
            3: ((wd, 4 * HC + FC, FC),),
        }[g]
        return [
            pltpu.make_async_copy(
                src.at[l], W.at[l, shard(a, b), pl.ds(first, width)], loc.at[l, 2 * g + place if g == 0 else g + 2]
            )
            for place, (src, first, width) in enumerate(parts)
        ]

    for l in range(2):
        for g in range(4):
            for copy in load_weight(l, g):
                copy.start()
    tok_copy = pltpu.make_async_copy(tok.at[0], STB, loc.at[0, 6])
    tok_copy.start()
    vectors = (gain_one, shift_one, out_b, gain_two, shift_two, down_b, query_b, value_b)
    for l in range(2):
        for place, vector in enumerate(vectors):
            RAW[dp, 12 * l + place : 12 * l + place + 1, 0:S] = vector[...].astype(f32)[l : l + 1, :]
        for q in range(4):
            RAW[dp, 12 * l + 8 + q : 12 * l + 9 + q, 0:S] = up_b[...].astype(f32)[l : l + 1, q * S : (q + 1) * S]
    pl.semaphore_wait(barrier, A + B + 1)

    def wrow(l, aa, bb, g):
        return W.at[l, shard(aa, bb), pl.ds(groups[g][0], groups[g][1])]

    def wz(l, g, k, source, device):
        ref = wrow(l, source, b, g)
        return remote(ref, ref, wz_s.at[l, g, k], wz_r.at[l, g, k], device)

    def wx(l, g, k, j, minor, device):
        ref = wrow(l, (a - k + A) % A, minor, g)
        return remote(ref, ref, wx_s.at[l, g, k, j], wx_r.at[l, g, k, j], device)

    def w_send_x(l, g, k):
        repeat(1, B, lambda j: wx(l, g, k, j, b, dp_dev(a, near(j))).start())

    def w_start(l, g):
        for copy in load_weight(l, g):
            copy.wait()
        repeat(1, A, lambda k: wz(l, g, k, a, dp_dev(far(k), b)).start())

    def w_pass(l, g, k):
        wz(l, g, k, (a - k + A) % A, dp_dev(far(k), b)).wait_recv()
        w_send_x(l, g, k)

    def w_pump(l, g, first=1, last=None):
        repeat(first, A if last is None else last + 1, lambda k: w_pass(l, g, k))

    def w_done(l, g):
        def one(k):
            repeat(1, B, lambda j: wx(l, g, k, j, (b - j + B) % B, dp_dev(a, near(j))).wait_recv())

        repeat(0, A, one)

    def w_sent(l, g):
        repeat(1, A, lambda k: wz(l, g, k, a, dp_dev(far(k), b)).wait_send())

        def one(k):
            repeat(1, B, lambda j: wx(l, g, k, j, b, dp_dev(a, near(j))).wait_send())

        repeat(0, A, one)

    def ag_copy(buf, kind):
        row = blk(t) if kind < 2 else blk(flip(2))
        return remote(buf.at[row], buf.at[row], ag_s.at[kind], ag_r.at[kind], ypeer if kind == 0 else sib)

    def ag_start(buf):
        ag_copy(buf, 0).start()
        ag_copy(buf, 1).start()

    def ag_wait(buf, i):
        @pl.when(i == 1)
        def _():
            ref = buf.at[blk(flip(1))]
            remote(ref, ref, ag_s.at[1], ag_r.at[1], sib).wait_recv()

        @pl.when(i == 2)
        def _():
            ref = buf.at[blk(flip(2))]
            remote(ref, ref, ag_s.at[0], ag_r.at[0], ypeer).wait_recv()
            ag_copy(buf, 2).start()

        @pl.when(i == 3)
        def _():
            ref = buf.at[blk(flip(3))]
            remote(ref, ref, ag_s.at[2], ag_r.at[2], sib).wait_recv()
            for kind in range(3):
                ag_copy(buf, kind).wait_send()

    rs_a = remote(SA, RA, rs_s.at[0], rs_r.at[0], sib)
    rs_b = remote(SB, RB, rs_s.at[1], rs_r.at[1], ypeer)
    rs_c = remote(SC, RC, rs_s.at[2], rs_r.at[2], sib)

    def rs_run(part, hooks={}):
        @pl.loop(0, 4)
        def _(step):
            for place, hook in hooks.items():
                pl.when(step == place)(hook)
            ACC[...] = part(flip(3 - step))

            @pl.when(step == 0)
            def _():
                SA[...] = ACC[...].astype(bf16)
                rs_a.start()

            @pl.when(step == 1)
            def _():
                rs_a.wait_recv()
                SB[...] = (ACC[...] + RA[...].astype(f32)).astype(bf16)
                rs_b.start()

            @pl.when(step == 2)
            def _():
                SC[...] = ACC[...].astype(bf16)
                rs_c.start()

    def rs_wait():
        rs_c.wait_recv()
        rs_b.wait_recv()

    def rs_sum(row):
        return ACC[row, :] + RB[row, :].astype(f32) + RC[row, :].astype(f32)

    def rs_end():
        rs_a.wait_send()
        rs_b.wait_send()
        rs_c.wait_send()

    def by_chunk(body):
        @pl.loop(0, R // CHUNK)
        def _(index):
            body(pl.ds(pl.multiple_of(index * CHUNK, CHUNK), CHUNK), pl.ds(pl.multiple_of(t * R + index * CHUNK, CHUNK), CHUNK))

    def head_mask(h):
        lane = lax.broadcasted_iota(jnp.int32, (R, HC), 1)
        return (lane >= h * HD) & (lane < (h + 1) * HD)

    def vz(k, source, device):
        ref = RAW.at[source * B + b]
        return remote(ref, ref, vz_s.at[k], vz_r.at[k], device)

    def vx(k, j, minor, device):
        ref = RAW.at[(a - k + A) % A * B + minor]
        return remote(ref, ref, vx_s.at[k, j], vx_r.at[k, j], device)

    def v_send_x(k):
        repeat(1, B, lambda j: vx(k, j, b, dp_dev(a, near(j))).start())

    def v_pass(k):
        vz(k, (a - k + A) % A, dp_dev(far(k), b)).wait_recv()
        v_send_x(k)

    def v_done(k):
        repeat(1, B, lambda j: vx(k, j, (b - j + B) % B, dp_dev(a, near(j))).wait_recv())

    def v_sent(k):
        repeat(1, B, lambda j: vx(k, j, b, dp_dev(a, near(j))).wait_send())

    repeat(1, A, lambda k: vz(k, a, dp_dev(far(k), b)).start())
    v_send_x(0)

    w_start(0, 0)
    w_send_x(0, 0, 0)
    tok_copy.wait()

    def load_tokens(row, full):
        X[0, row, :] = STB[row, :].astype(f32)

    by_chunk(load_tokens)
    for g in range(1, 4):
        w_start(0, g)
        w_send_x(0, g, 0)
    for g in range(4):
        w_start(1, g)
    repeat(1, A, v_pass)
    repeat(0, A, v_done)
    repeat(1, A, lambda k: vz(k, a, dp_dev(far(k), b)).wait_send())
    repeat(0, A, v_sent)

    quarter = A * B // 4

    def lay_out(row, offset, pieces):
        per_tile = max(1, 128 // S)
        for start in range(0, len(pieces), per_tile):
            run = pieces[start : start + per_tile]
            value = run[0] if len(run) == 1 else jnp.concatenate([piece[:, 0:S] for piece in run], axis=1)
            at = offset + start * S
            vec[row[0], row[1] : row[1] + 1, at : at + len(run) * S] = value[:, 0 : len(run) * S]

    for l in range(2):
        for place in range(6):
            lay_out((l, place), 0, [RAW[d, 12 * l + place : 12 * l + place + 1, :] for d in range(A * B)])
        for place in range(2):
            lay_out(
                (l, 7), place * HC,
                [RAW[t * quarter + d, 12 * l + 6 + place : 12 * l + 7 + place, :] for d in range(quarter)],
            )
        lay_out(
            (l, 6), 0,
            [RAW[t * quarter + d, 12 * l + 8 + q : 12 * l + 9 + q, :] for d in range(quarter) for q in range(4)],
        )

    spills = [
        pltpu.make_async_copy(
            W.at[0, :, pl.ds(first, width)], spill.at[:, pl.ds(first, width)], loc.at[1, 6 + g]
        )
        for g, (first, width) in enumerate(groups)
    ]

    for l in range(2):

        def first_norm(row, full):
            n, _ = norm_parts(X[l, row, :])
            NF[l, full, :] = (n * vec[l, 0:1, :] + vec[l, 1:2, :]).astype(bf16)

        by_chunk(first_norm)
        ag_start(NF.at[l])
        if l == 0:
            w_pump(0, 0)
        w_pump(l, 1)
        if l == 0:
            w_send_x(1, 0, 0)
            w_send_x(1, 1, 0)
        w_done(l, 0)

        @pl.loop(0, 4)
        def _(i):
            ag_wait(NF.at[l], i)
            row = blk(flip(i))
            out = dot_nn(NF[l, row, :], W[l, :, 0 : 3 * HC])
            QKV[l, row, 0:HC] = (out[:, 0:HC] + vec[l, 7:8, 0:HC]).astype(bf16)
            QKV[l, row, HC : 2 * HC] = out[:, HC : 2 * HC].astype(bf16)
            QKV[l, row, 2 * HC : 3 * HC] = (out[:, 2 * HC : 3 * HC] + vec[l, 7:8, HC : 2 * HC]).astype(bf16)

        VT[...] = QKV[l, :, 2 * HC : 3 * HC].T
        w_done(l, 1)

        def attend(i):
            row = blk(i)
            queries = QKV[l, row, 0:HC]
            keys = QKV[l, :, HC : 2 * HC]
            outs = []
            for h in range(heads):
                masked = jnp.where(head_mask(h), queries, jnp.zeros_like(queries))
                scores = dot_nt(keys, masked) * (score_scale * LOG2E)
                top = jnp.max(scores, axis=0, keepdims=True)
                exps = jnp.exp2(scores - top)
                total = jnp.sum(exps, axis=0, keepdims=True)
                LSE[l, h : h + 1, row] = top + jnp.log(total) * LOG2E
                outs.append(dot_nn(VT[h * HD : (h + 1) * HD, :], exps.astype(bf16)) * (1.0 / total))
            AT[l, row, :] = jnp.concatenate(outs, axis=0).T.astype(bf16)
            return dot_nt(AT[l, row, :], W[l, :, 3 * HC : 4 * HC])

        rs_run(attend, {2: lambda: w_pass(l, 2, 1), 3: lambda: w_pump(l, 2, 2, A - 2)})
        w_pass(l, 2, A - 1)
        rs_wait()

        def second_norm(row, full):
            middle = X[l, row, :] + rs_sum(row) + vec[l, 2:3, :]
            MID[l, row, :] = middle
            n, _ = norm_parts(middle)
            NF2[l, full, :] = (n * vec[l, 3:4, :] + vec[l, 4:5, :]).astype(bf16)

        by_chunk(second_norm)
        rs_end()
        ag_start(NF2.at[l])
        w_done(l, 2)
        w_pass(l, 3, 1)

        @pl.loop(0, 4)
        def _(i):
            @pl.when(i == 2)
            def _():
                w_pump(l, 3, 2, A - 2)

            ag_wait(NF2.at[l], i)
            row = blk(flip(i))
            pre = dot_nn(NF2[l, row, :], W[l, :, 4 * HC : 4 * HC + FC]) + vec[l, 6:7, :]
            cumul = 0.5 * (1.0 + lax.erf(pre * ROOT_HALF))
            ACT[l, row, :] = (pre * cumul).astype(bf16)
            GP[l, row, :] = (cumul + pre * (jnp.exp(-0.5 * pre * pre) * PHI_ZERO)).astype(bf16)

        w_pass(l, 3, A - 1)
        if l == 0:
            w_send_x(1, 2, 0)
            w_send_x(1, 3, 0)
        w_done(l, 3)
        rs_run(lambda i: dot_nt(ACT[l, blk(i), :], W[l, :, 4 * HC + FC : 4 * HC + 2 * FC]))
        if l == 0:
            w_pass(1, 0, 1)
            w_pump(1, 0, 2, A - 2)
        rs_wait()

        def layer_out(row, full):
            out = MID[l, row, :] + rs_sum(row) + vec[l, 5:6, :]
            if l == 0:
                X[1, row, :] = out
            else:
                STB[row, :] = out.astype(bf16)

        by_chunk(layer_out)
        rs_end()
        if l == 0:
            w_pass(1, 0, A - 1)
            for g in range(4):
                w_sent(0, g)
            for copy in spills:
                copy.start()

    mixed_copy = pltpu.make_async_copy(STB, mixed.at[0], loc.at[0, 6])
    mixed_copy.start()
    for g in range(4):
        w_sent(1, g)
    for copy in spills:
        copy.wait()
    mixed_copy.wait()
    cot_copy = pltpu.make_async_copy(cot.at[0], STB, loc.at[0, 7])
    cot_copy.start()
    cot_copy.wait()
    live = counts[0].astype(f32)

    def load_cot(row, full):
        GC[row, :] = STB[row, :].astype(f32) * live

    by_chunk(load_cot)
    vg[...] = jnp.zeros_like(vg)

    def gsrc(l, g):
        first, width = groups[g]
        if l == 1:
            return W, 0, first, width
        if g == 3:
            return ACT, 1, 0, width
        if g == 2:
            return GP, 1, 0, width
        return NF2, 1, (0 if g == 0 else 3 * HC), width

    def gref(l, g, aa, bb):
        buf, slot, first, width = gsrc(l, g)
        return buf.at[slot, shard(aa, bb), pl.ds(first, width)]

    def gb(l, g, j, aa):
        first, width = groups[g]
        return remote(
            gref(l, g, aa, near(j)), BR.at[j - 1, aa, :, pl.ds(first, width)], gb_s.at[l, g, j, aa], gb_r.at[l, g, j, aa],
            dp_dev(a, near(j)),
        )

    def ga(l, g, k):
        first, width = groups[g]
        return remote(
            gref(l, g, far(k), b), AR.at[k - 1, :, pl.ds(first, width)], ga_s.at[l, g, k], ga_r.at[l, g, k], dp_dev(far(k), b)
        )

    def g_start(l, g):
        if l == 0:
            pl.semaphore_wait(cred_b.at[g], B - 1)

        def one(k):
            repeat(1, B, lambda j: gb(l, g, j, far(k)).start())

        repeat(1, A + 1, one)

    def g_piece(l, g, aa):
        first, width = groups[g]
        repeat(1, B, lambda j: gb(l, g, j, aa).wait_recv())
        total = gref(l, g, aa, b)[...].astype(f32)
        for j in range(1, B):
            total = total + BR[j - 1, aa, :, first : first + width].astype(f32)
        return total

    def g_pass(l, g, k):
        piece = gref(l, g, far(k), b)
        piece[...] = g_piece(l, g, far(k)).astype(bf16)
        ga(l, g, k).start()

    def g_pump(l, g, first=1, last=None):
        if l == 0 and first == 1:
            pl.semaphore_wait(cred_a.at[g], A - 1)
        repeat(first, A if last is None else last + 1, lambda k: g_pass(l, g, k))

    def g_own(l, g):
        first, width = groups[g]
        OST[l, :, first : first + width] = g_piece(l, g, a)
        if l == 1:
            repeat(
                1, B,
                lambda j: pl.semaphore_signal(cred_b.at[g], inc=1, device_id=dp_dev(a, near(j)), device_id_type=MESH),
            )

    def g_out(l, g):
        parts = {0: ((gq, 0, HC), (gk, HC, HC), (gv, 2 * HC, HC)), 1: ((go, 0, HC),), 2: ((gu, 0, FC),), 3: ((gd, 0, FC),)}[g]
        first = groups[g][0]
        return [
            pltpu.make_async_copy(
                OST.at[l, :, pl.ds(first + at, width)], dst.at[l], loc.at[l, 2 * g + place if g == 0 else g + 2]
            )
            for place, (dst, at, width) in enumerate(parts)
        ]

    def g_final(l, g):
        first, width = groups[g]

        def one(k):
            ga(l, g, k).wait_recv()
            OST[l, :, first : first + width] += AR[k - 1, :, first : first + width].astype(f32)

        repeat(1, A, one)
        if l == 1:
            repeat(
                1, A,
                lambda k: pl.semaphore_signal(cred_a.at[g], inc=1, device_id=dp_dev(far(k), b), device_id_type=MESH),
            )
        for copy in g_out(l, g):
            copy.start()

    def g_sent(l, g):
        repeat(1, A, lambda k: ga(l, g, k).wait_send())

        def one(k):
            repeat(1, B, lambda j: gb(l, g, j, far(k)).wait_send())

        repeat(1, A + 1, one)
        for copy in g_out(l, g):
            copy.wait()

    def weight_grad(l, g, left, right):
        buf, slot, first, width = gsrc(l, g)

        @pl.loop(0, D // R)
        def _(i):
            buf[slot, blk(i), first : first + width] = dot_tn(left[:, blk(i)], right[...]).astype(bf16)

        g_start(l, g)

    def reload(g):
        first, width = groups[g]
        return pltpu.make_async_copy(spill.at[:, pl.ds(first, width)], W.at[1, :, pl.ds(first, width)], loc.at[1, 6 + g])

    def vgx(l, j):
        return remote(vg.at[l], VGX.at[l, j - 1], vgx_s.at[l, j], vgx_r.at[l, j], dp_dev(a, near(j)))

    def vgz(l, k):
        return remote(VGS.at[l], VGZ.at[l, k - 1], vgz_s.at[l, k], vgz_r.at[l, k], dp_dev(far(k), b))

    def vgt(l, i):
        return remote(VGU.at[l], VGT.at[l, i - 1], vgt_s.at[l, i], vgt_r.at[l, i], (dp, flip(i)))

    def vg_near(l):
        repeat(1, B, lambda j: vgx(l, j).start())

    def vg_far(l):
        repeat(1, B, lambda j: vgx(l, j).wait_recv())
        VGS[l] = vg[l]
        for j in range(1, B):
            VGS[l] += VGX[l, j - 1]
        repeat(1, A, lambda k: vgz(l, k).start())

    def vg_tensor(l):
        repeat(1, A, lambda k: vgz(l, k).wait_recv())
        VGU[l] = VGS[l]
        for k in range(1, A):
            VGU[l] += VGZ[l, k - 1]
        repeat(1, 4, lambda i: vgt(l, i).start())

    def own_lanes(ref, start):
        if S % 128 == 0:
            return ref[:, pl.ds(pl.multiple_of(start, 128), S)]
        tile = ref[:, pl.ds(pl.multiple_of(start // 128 * 128, 128), 128)]
        return pltpu.roll(tile, (128 - start % 128) % 128, 1)[:, 0:S]

    def vg_end(l):
        repeat(1, 4, lambda i: vgt(l, i).wait_recv())
        owner = dp // quarter
        total = VGU[l]
        picked = jnp.where(flip(0) == owner, VGU[l], 0.0)
        for i in range(1, 4):
            total = total + VGT[l, i - 1]
            picked = picked + jnp.where(flip(i) == owner, VGT[l, i - 1], 0.0)
        TOT[0:8, :] = total
        TOT[8:16, :] = picked
        inside = dp % quarter
        VS[l, 0:6, 0:S] = own_lanes(TOT.at[0:8], dp * S)[0:6, :]
        VS[l, 6:7, 0:S] = own_lanes(TOT.at[8:16], inside * S)[7:8, :]
        VS[l, 7:8, 0:S] = own_lanes(TOT.at[8:16], HC + inside * S)[7:8, :]
        for q in range(4):
            VS[l, 8 + q : 9 + q, 0:S] = own_lanes(TOT.at[8:16], inside * 4 * S + q * S)[6:7, :]
        repeat(1, B, lambda j: vgx(l, j).wait_send())
        repeat(1, A, lambda k: vgz(l, k).wait_send())
        repeat(1, 4, lambda i: vgt(l, i).wait_send())

    for l in (1, 0):

        def low_grad(row, full):
            low = GC[row, :].astype(bf16)
            GF[full, :] = low
            vg[l, 5:6, :] += jnp.sum(low.astype(f32), axis=0, keepdims=True)

        by_chunk(low_grad)
        ag_start(GF)
        if l == 0:
            reload(3).wait()
            reload(2).wait()
            g_own(1, 1)
            g_pass(1, 0, 1)

        @pl.loop(0, 4)
        def _(i):
            if l == 0:

                @pl.when(i == 2)
                def _():
                    g_pump(1, 0, 2, A - 2)

            ag_wait(GF, i)
            row = blk(flip(i))
            act_grad = dot_nn(GF[row, :], W[1, :, 4 * HC + FC : 4 * HC + 2 * FC])
            pre_grad = (act_grad * GP[l, row, :].astype(f32)).astype(bf16)
            GP[l, row, :] = pre_grad
            vg[l, 6:7, :] += jnp.sum(pre_grad.astype(f32), axis=0, keepdims=True)

        if l == 0:
            g_pass(1, 0, A - 1)
            vg_far(1)
        rs_run(lambda i: dot_nt(GP[l, blk(i), :], W[1, :, 4 * HC : 4 * HC + FC]))
        if l == 1:
            reload(2).start()
            reload(3).start()
        if l == 0:
            g_own(1, 0)
        weight_grad(l, 3, GF, ACT.at[l])
        weight_grad(l, 2, NF2.at[l], GP.at[l])
        if l == 0:
            vg_tensor(1)
        rs_wait()

        def second_back(row, full):
            dy = rs_sum(row)
            n, scale = norm_parts(MID[l, row, :])
            vg[l, 3:4, :] += jnp.sum(dy * n, axis=0, keepdims=True)
            vg[l, 4:5, :] += jnp.sum(dy, axis=0, keepdims=True)
            dn = dy * vec[l, 3:4, :]
            part = scale * (
                dn - jnp.mean(dn, axis=-1, keepdims=True) - n * jnp.mean(dn * n, axis=-1, keepdims=True)
            )
            grad = GC[row, :] + part
            GC[row, :] = grad
            low = grad.astype(bf16)
            MF[full, :] = low
            vg[l, 2:3, :] += jnp.sum(low.astype(f32), axis=0, keepdims=True)

        by_chunk(second_back)
        rs_end()
        ag_start(MF)
        if l == 0:
            g_final(1, 2)
            g_final(1, 1)
            reload(1).wait()
            reload(0).wait()
        g_pump(l, 3, 1, A - 2)

        @pl.loop(0, 4)
        def _(i):
            ag_wait(MF, i)
            row = blk(flip(i))
            DO[row, :] = dot_nn(MF[row, :], W[1, :, 3 * HC : 4 * HC]).astype(bf16)

        weight_grad(l, 1, MF, AT.at[l])
        if l == 0:
            g_final(1, 0)
        g_pass(l, 3, A - 1)
        if l == 1:
            reload(1).start()
        KT[...] = QKV[l, :, HC : 2 * HC].T
        DKA[...] = jnp.zeros_like(DKA)
        DVA[...] = jnp.zeros_like(DVA)

        @pl.loop(0, 4)
        def _(i):
            @pl.when(i == 1)
            def _():
                g_own(l, 3)

            @pl.when(i == 3)
            def _():
                g_pump(l, 2, 1, 1)

            row = blk(i)
            queries = QKV[l, row, 0:HC]
            keys = QKV[l, :, HC : 2 * HC]
            values = QKV[l, :, 2 * HC : 3 * HC]
            out_grads = DO[row, :]
            parts = []
            for h in range(heads):
                mask = head_mask(h)
                q_one = jnp.where(mask, queries, jnp.zeros_like(queries))
                do_one = jnp.where(mask, out_grads, jnp.zeros_like(out_grads))
                probs = jnp.exp2(dot_nt(keys, q_one) * (score_scale * LOG2E) - LSE[l, h : h + 1, row])
                prob_grad = dot_nt(values, do_one)
                DVA[...] += dot_nn(probs.astype(bf16), do_one)
                row_dot = jnp.sum(probs * prob_grad, axis=0, keepdims=True)
                score_grad = (probs * (prob_grad - row_dot)).astype(bf16)
                DKA[...] += dot_nn(score_grad, q_one)
                parts.append(dot_nn(KT[h * HD : (h + 1) * HD, :], score_grad))
            DQKV[row, 0:HC] = (jnp.concatenate(parts, axis=0).T * score_scale).astype(bf16)

        g_pump(l, 2, 2, A - 2)
        DQKV[:, HC : 2 * HC] = (DKA[...] * score_scale).astype(bf16)
        DQKV[:, 2 * HC : 3 * HC] = DVA[...].astype(bf16)
        rs_run(lambda i: dot_nt(DQKV[blk(i), :], W[1, :, 0 : 3 * HC]))
        if l == 1:
            reload(0).start()
        weight_grad(l, 0, NF.at[l], DQKV)
        vg[l, 7:8, 0:HC] = jnp.sum(DQKV[:, 0:HC].astype(f32), axis=0, keepdims=True)
        vg[l, 7:8, HC : 2 * HC] = jnp.sum(DQKV[:, 2 * HC : 3 * HC].astype(f32), axis=0, keepdims=True)
        g_pass(l, 2, A - 1)
        g_own(l, 2)
        g_final(l, 3)
        if l == 0:
            vg_end(1)
        rs_wait()

        def first_back(row, full):
            dy = rs_sum(row)
            n, scale = norm_parts(X[l, row, :])
            vg[l, 0:1, :] += jnp.sum(dy * n, axis=0, keepdims=True)
            vg[l, 1:2, :] += jnp.sum(dy, axis=0, keepdims=True)
            dn = dy * vec[l, 0:1, :]
            part = scale * (
                dn - jnp.mean(dn, axis=-1, keepdims=True) - n * jnp.mean(dn * n, axis=-1, keepdims=True)
            )
            GC[row, :] = GC[row, :] + part

        by_chunk(first_back)
        rs_end()
        vg_near(l)
        if l == 1:
            g_pump(1, 1)

    grad_copy = pltpu.make_async_copy(GC, tgrad.at[0], loc.at[0, 7])
    grad_copy.start()
    g_pump(0, 1)
    vg_far(0)
    g_own(0, 1)
    g_pump(0, 0)
    vg_tensor(0)
    g_final(0, 2)
    g_final(0, 1)
    g_own(0, 0)
    vg_end(0)
    vs_copy = pltpu.make_async_copy(VS, vs_out, loc.at[0, 6])
    vs_copy.start()
    g_final(0, 0)
    grad_copy.wait()
    vs_copy.wait()
    for l in range(2):
        for g in range(4):
            g_sent(l, g)


def finish_kernel(S, *refs):
    sources, small, targets, smalls, stages, sems = refs[:8], refs[8], refs[9:17], refs[17:26], refs[26:34], refs[34]
    arrivals = [
        pltpu.make_async_copy(source, stage, sems.at[0, at]) for at, (source, stage) in enumerate(zip(sources, stages))
    ]
    copies = [
        pltpu.make_async_copy(stage, target, sems.at[1, at]) for at, (stage, target) in enumerate(zip(stages, targets))
    ]
    for arrival in arrivals:
        arrival.start()
    for arrival, copy in zip(arrivals, copies):
        arrival.wait()
        copy.start()
    for l in range(2):
        for place in range(8):
            smalls[place][l : l + 1, :] = small[l, place : place + 1, 0:S]
        for q in range(4):
            smalls[8][l : l + 1, q * S : (q + 1) * S] = small[l, 8 + q : 9 + q, 0:S]
    for copy in copies:
        copy.wait()


def shards(
    mesh_dp,
    tokens, clip_counts, cotangent, norm1_gain, norm1_shift, w_query, query_bias, w_key, w_value, value_bias, w_out,
    out_bias, norm2_gain, norm2_shift, w_up, up_bias, w_down, down_bias,
):
    layers, S, HC = w_query.shape
    FC = w_up.shape[2]
    _, R, D = tokens.shape
    B = 1
    while 4 * B * B <= mesh_dp:
        B *= 2
    A = mesh_dp // B
    LEN = 4 * R
    COLS = 4 * HC + 2 * FC
    dims = (A, B, S, R, D, HC, FC)
    vm = pltpu.VMEM
    dma = pltpu.SemaphoreType.DMA
    any_spec = pl.BlockSpec(memory_space=pl.ANY)
    vmem_spec = pl.BlockSpec(memory_space=pltpu.VMEM)
    grad_small = jax.ShapeDtypeStruct((layers, S, HC), f32)
    grad_large = jax.ShapeDtypeStruct((layers, S, FC), f32)
    outs = pl.pallas_call(
        functools.partial(encoder_kernel, dims),
        out_shape=(
            jax.ShapeDtypeStruct((1, R, D), bf16),
            jax.ShapeDtypeStruct((1, R, D), f32),
            grad_small, grad_small, grad_small, grad_small, grad_large, grad_large,
            jax.ShapeDtypeStruct((layers, 16, 128), f32),
            jax.ShapeDtypeStruct((D, COLS), bf16),
        ),
        in_specs=[any_spec, any_spec, pl.BlockSpec(memory_space=pltpu.SMEM)] + [any_spec] * 6 + [vmem_spec] * 9,
        out_specs=tuple([any_spec] * 10),
        scratch_shapes=[
            vm((2, D, COLS), bf16),
            vm((2, LEN, D), bf16),
            vm((2, LEN, 3 * HC), bf16),
            vm((2, LEN, HC), bf16),
            vm((2, 8, LEN), f32),
            vm((2, R, D), f32),
            vm((2, R, D), f32),
            vm((2, LEN, D), bf16),
            vm((2, LEN, FC), bf16),
            vm((2, LEN, FC), bf16),
            vm((LEN, D), bf16),
            vm((LEN, D), bf16),
            vm((LEN, 3 * HC), bf16),
            vm((LEN, HC), bf16),
            vm((R, D), f32),
            vm((max(B - 1, 1), A, S, COLS), bf16),
            vm((max(A - 1, 1), S, COLS), bf16),
            vm((R, D), bf16), vm((R, D), bf16), vm((R, D), bf16),
            vm((R, D), bf16), vm((R, D), bf16), vm((R, D), bf16),
            vm((R, D), f32),
            vm((2, S, COLS), f32),
            vm((HC, LEN), bf16), vm((HC, LEN), bf16),
            vm((LEN, HC), f32), vm((LEN, HC), f32),
            vm((R, D), bf16),
            vm((A * B, 24, 128), f32),
            vm((2, 8, D), f32), vm((2, 8, D), f32),
            vm((2, max(B - 1, 1), 8, D), f32),
            vm((2, 8, D), f32),
            vm((2, max(A - 1, 1), 8, D), f32),
            vm((2, 8, D), f32),
            vm((2, 3, 8, D), f32),
            vm((2, 16, 128), f32),
            vm((16, D), f32),
            dma((2, 10)),
            dma((3,)), dma((3,)), dma((3,)), dma((3,)),
            dma((2, 4, A)), dma((2, 4, A)), dma((2, 4, A, B)), dma((2, 4, A, B)),
            dma((2, 4, B, A)), dma((2, 4, B, A)), dma((2, 4, A)), dma((2, 4, A)),
            dma((A,)), dma((A,)), dma((A, B)), dma((A, B)),
            dma((2, B)), dma((2, B)), dma((2, A)), dma((2, A)), dma((2, 4)), dma((2, 4)),
            pltpu.SemaphoreType.REGULAR((4,)), pltpu.SemaphoreType.REGULAR((4,)),
        ],
        compiler_params=pltpu.CompilerParams(
            collective_id=0, has_side_effects=True, vmem_limit_bytes=64 * 2**20 - 2**17
        ),
        name="encoder",
    )(tokens, cotangent, clip_counts, w_query, w_key, w_value, w_out, w_up, w_down, norm1_gain, norm1_shift,
      out_bias, norm2_gain, norm2_shift, down_bias, query_bias, value_bias, up_bias)

    small = jax.ShapeDtypeStruct((layers, S), f32)
    large_types = tuple(jax.ShapeDtypeStruct(member.shape, member.dtype) for member in outs[:8])
    (mixed, tokens_grad, gq, gk, gv, go, gu, gd, g_gain_one, g_shift_one, g_out, g_gain_two, g_shift_two, g_down, g_query,
     g_value, g_up) = pl.pallas_call(
        functools.partial(finish_kernel, S),
        out_shape=large_types + (small,) * 8 + (jax.ShapeDtypeStruct((layers, 4 * S), f32),),
        in_specs=[any_spec] * 8 + [vmem_spec],
        out_specs=tuple([any_spec] * 8 + [vmem_spec] * 9),
        scratch_shapes=[vm(member.shape, member.dtype) for member in outs[:8]] + [dma((2, 8))],
        compiler_params=pltpu.CompilerParams(vmem_limit_bytes=64 * 2**20 - 2**17),
        name="finish",
    )(*outs[:9])
    return (
        mixed, tokens_grad, g_gain_one, g_shift_one, gq, g_query, gk, gv, g_value, go, g_out, g_gain_two, g_shift_two, gu,
        g_up, gd, g_down,
    )


def solution(mesh):
    rows = P("dp", "tensor", None)
    vector = P(None, "dp")
    matrix = P(None, "dp", "tensor")
    return jax.shard_map(
        functools.partial(shards, mesh.shape["dp"]),
        mesh=mesh,
        in_specs=(
            rows, P("dp"), rows, vector, vector, matrix, vector, matrix, matrix, vector, matrix, vector, vector, vector,
            matrix, vector, matrix, vector,
        ),
        out_specs=(
            rows, rows, vector, vector, matrix, vector, matrix, matrix, vector, matrix, vector, vector, vector, matrix,
            vector, matrix, vector,
        ),
        check_vma=False,
    )
```

```python
import functools
import math

import jax
import jax.numpy as jnp
from jax import lax
from jax.experimental import pallas as pl
from jax.experimental.pallas import tpu as pltpu
from jax.sharding import PartitionSpec as P

HD = 64
norm_eps = 1e-06
MESH = pl.DeviceIdType.MESH
bf16 = jnp.bfloat16
f32 = jnp.float32
ROOT_HALF = 1.0 / math.sqrt(2.0)
PHI_ZERO = 1.0 / math.sqrt(2.0 * math.pi)
LOG2E = 1.0 / math.log(2.0)
CHUNK = 64
SCHEDULE = (0, 16, 4, 16, 20, 20, 24, 28, 36, 40, 44, 48, 48, 52, 52, 56, 60, 60, 64, 64, 76, 80, 92, 96, 32, 72)


def dot_nn(left, right):
    return jnp.dot(left, right, preferred_element_type=f32)


def dot_nt(left, right):
    return lax.dot_general(left, right, (((1,), (1,)), ((), ())), preferred_element_type=f32)


def dot_tn(left, right):
    return lax.dot_general(left, right, (((0,), (0,)), ((), ())), preferred_element_type=f32)


def repeat(low, high, body):
    if high - low <= 4:
        for index in range(low, high):
            body(index)
    else:

        pl.loop(low, high)(body)


def norm_parts(rows):
    centered = rows - jnp.mean(rows, axis=-1, keepdims=True)
    scale = lax.rsqrt(jnp.mean(centered * centered, axis=-1, keepdims=True) + norm_eps)
    return centered * scale, scale


def encoder_kernel(
    dims,
    tok, cot, counts, wq, wk, wv, wo, wu, wd, gain_one, shift_one, out_b, gain_two, shift_two, down_b, query_b, value_b, up_b,
    mixed, tgrad, gq, gk, gv, go, gu, gd, vs_out, spill,
    W, NF, QKV, AT, LSE, X, MID, NF2, ACT, GP, GF, MF, DQKV, GC, BR, AR,
    SA, SB, SC, RA, RB, RC, ACC, PBUF, OST, TR, DKA, STB, RAW, vec, vg, VGX, VGS, VGZ, VGU, VGT, VS, TOT,
    loc, ag_s, ag_r, rs_s, rs_r, wz_s, wz_r, wx_s, wx_r, gb_s, gb_r, ga_s, ga_r,
    vz_s, vz_r, vx_s, vx_r, vgx_s, vgx_r, vgz_s, vgz_r, vgt_s, vgt_r, cred_b, cred_a, ack,
):
    A, B, S, R, D, HC, FC = dims
    heads = HC // HD
    score_scale = HD ** (-0.5)
    dp = lax.axis_index("dp")
    t = lax.axis_index("tensor")
    a = dp // B
    b = dp % B
    y = t // 2
    c = t % 2

    def flip(i):
        return 2 * ((y + i // 2) % 2) + (c + i % 2) % 2

    sib = (dp, flip(1))
    ypeer = (dp, flip(2))
    corner = (dp, flip(3))

    def dp_dev(aa, bb):
        return (aa * B + bb, t)

    def far(k):
        return (a + k) % A

    def near(j):
        return (b + j) % B

    fine = A * B <= 16
    spans = {"qkv": (0, 3 * HC), "out": (3 * HC, HC), "up": (4 * HC, FC), "down": (4 * HC + FC, FC)}
    groups, sets = [], {}
    for name, (first, width) in spans.items():
        step = HC if fine else width
        sets[name] = tuple(range(len(groups), len(groups) + width // step))
        groups.extend((at, step) for at in range(first, first + width, step))

    def part(pieces, low, high, parts):
        return pieces[low * len(pieces) // parts : high * len(pieces) // parts]

    half = R // 2
    quarter = A * B // 4

    def own_half(h):
        return pl.ds(pl.multiple_of(h * half, half), half)

    def hrow(i, h):
        return pl.ds(pl.multiple_of(i * R + h * half, half), half)

    def near_pair(h):
        return hrow(flip(1), h), hrow(flip(0), h)

    def far_pair(h):
        return hrow(flip(3), h), hrow(flip(2), h)

    def pair(near, h):
        return hrow(flip(3 - 2 * near), h), hrow(flip(2 - 2 * near), h)

    def both(ref, rows):
        return jnp.concatenate([ref[rows[0], :], ref[rows[1], :]], axis=0)

    def put(ref, rows, value):
        ref[rows[0], :] = value[0:half]
        ref[rows[1], :] = value[half : 2 * half]

    def blk(i):
        return pl.ds(pl.multiple_of(i * R, R), R)

    def shard(aa, bb):
        return pl.ds(pl.multiple_of((aa * B + bb) * S, S), S)

    def remote(src, dst, send, recv, device):
        return pltpu.make_async_remote_copy(
            src_ref=src, dst_ref=dst, send_sem=send, recv_sem=recv, device_id=device, device_id_type=MESH
        )

    barrier = pltpu.get_barrier_semaphore()

    def greet(device):
        pl.semaphore_signal(barrier, inc=1, device_id=device, device_id_type=MESH)

    greet(sib)
    greet(ypeer)
    greet(corner)
    repeat(1, A, lambda k: greet(dp_dev(far(k), b)))
    repeat(1, B, lambda j: greet(dp_dev(a, near(j))))

    weights = (
        (wq, 0, HC), (wk, HC, HC), (wv, 2 * HC, HC), (wo, 3 * HC, HC), (wu, 4 * HC, FC), (wd, 4 * HC + FC, FC),
    )
    loads = {
        (l, at): pltpu.make_async_copy(src.at[l], W.at[l, shard(a, b), pl.ds(first, width)], loc.at[l, at])
        for l in range(2)
        for at, (src, first, width) in enumerate(weights)
    }
    for copy in loads.values():
        copy.start()
    tok_copy = pltpu.make_async_copy(tok.at[0], STB, loc.at[0, 6])
    tok_copy.start()
    cot_copy = pltpu.make_async_copy(cot.at[0], STB, loc.at[0, 7])
    live = counts[0].astype(f32)
    vg[...] = jnp.zeros_like(vg)
    vectors = (gain_one, shift_one, out_b, gain_two, shift_two, down_b, query_b, value_b)
    for l in range(2):
        for place, vector in enumerate(vectors):
            RAW[dp, 12 * l + place : 12 * l + place + 1, 0:S] = vector[...].astype(f32)[l : l + 1, :]
        for q in range(4):
            RAW[dp, 12 * l + 8 + q : 12 * l + 9 + q, 0:S] = up_b[...].astype(f32)[l : l + 1, q * S : (q + 1) * S]
    pl.semaphore_wait(barrier, A + B + 1)

    order = [(l, g) for l in range(2) for g in range(len(groups))]

    def wrow(n, source, minor):
        l, g = order[n]
        return W.at[l, shard(source, minor), pl.ds(groups[g][0], groups[g][1])]

    def wz(n, way, hop, source):
        ref = wrow(n, source, b)
        return remote(ref, ref, wz_s.at[n, way, hop], wz_r.at[n, way, hop], dp_dev(a + 1 - 2 * way, b))

    def wx(n, behind, j, minor):
        ref = wrow(n, (a - behind + A) % A, minor)
        return remote(ref, ref, wx_s.at[n, behind, j], wx_r.at[n, behind, j], dp_dev(a, near(j)))

    def w_send_x(n, behind):
        repeat(1, B, lambda j: wx(n, behind, j, b).start())

    def w_arrive(n, hop):
        @pl.when(a >= hop)
        def _():
            wz(n, 0, hop, a - hop).wait_recv()
            if hop < A - 1:
                pl.when(a < A - 1)(lambda: wz(n, 0, hop + 1, a - hop).start())
            w_send_x(n, hop)

        @pl.when(a + hop < A)
        def _():
            wz(n, 1, hop, a + hop).wait_recv()
            if hop < A - 1:
                pl.when(a > 0)(lambda: wz(n, 1, hop + 1, a + hop).start())
            w_send_x(n, A - hop)

    progress = {"wave": 0, "line": 0, "own": 0, "load": 0}

    def w_wave():
        wave = progress["wave"]
        for n in range(progress["line"], min(wave + 3, len(order))):
            l, g = order[n]
            first = groups[g][0]
            for at, (_, place, wide) in enumerate(weights):
                if first <= place < first + groups[g][1]:
                    loads[l, at].wait()
            pl.when(a < A - 1)(lambda: wz(n, 0, 1, a).start())
            pl.when(a > 0)(lambda: wz(n, 1, 1, a).start())
            progress["line"] = n + 1
        for n in range(progress["own"], min(wave + 6, progress["line"] + 3, len(order))):
            if n < progress["line"]:
                w_send_x(n, 0)
                progress["own"] = n + 1
        for hop in range(1, A):
            if 0 <= wave - hop + 1 < len(order):
                w_arrive(wave - hop + 1, hop)
        progress["wave"] = wave + 1

    def w_pass(l, name, count=4, parts=4):
        chosen = part(sets[name], 0, count, parts)
        if chosen:
            while progress["wave"] < order.index((l, chosen[-1])) + A - 1:
                w_wave()

    def w_done(l, name):
        def one(n, behind):
            repeat(1, B, lambda j: wx(n, behind, j, (b - j + B) % B).wait_recv())

        for g in sets[name]:
            repeat(0, A, functools.partial(one, order.index((l, g))))

    def w_sent(l, g):
        n = order.index((l, g))
        pl.when(a < A - 1)(lambda: wz(n, 0, 1, a).wait_send())
        pl.when(a > 0)(lambda: wz(n, 1, 1, a).wait_send())
        for hop in range(1, A - 1):
            pl.when((a >= hop) & (a < A - 1))(lambda: wz(n, 0, hop + 1, a - hop).wait_send())
            pl.when((a + hop < A) & (a > 0))(lambda: wz(n, 1, hop + 1, a + hop).wait_send())

        def one(behind):
            repeat(1, B, lambda j: wx(n, behind, j, b).wait_send())

        repeat(0, A, one)

    def ag_copy(buf, h, kind, early=0):
        row = hrow(flip(2), h) if kind == 2 else hrow(t, h)
        send, recv = ag_s.at[early, h, kind], ag_r.at[early, h, kind]
        return remote(buf.at[row], buf.at[row], send, recv, ypeer if kind == 0 else sib)

    def ag_arrival(buf, h, kind, early=0):
        row = hrow(flip((2, 1, 3)[kind]), h)
        send, recv = ag_s.at[early, h, kind], ag_r.at[early, h, kind]
        return remote(buf.at[row], buf.at[row], send, recv, ypeer if kind == 0 else sib)

    def ag_start(buf, h, early=0):
        ag_copy(buf, h, 0, early).start()
        ag_copy(buf, h, 1, early).start()

    def ag_near(buf, h, early=0):
        ag_arrival(buf, h, 1, early).wait_recv()

    def ag_far(buf, h, early=0):
        ag_arrival(buf, h, 0, early).wait_recv()
        ag_copy(buf, h, 2, early).start()
        ag_arrival(buf, h, 2, early).wait_recv()
        for kind in range(3):
            ag_copy(buf, h, kind, early).wait_send()

    def rs_copy(h, kind):
        row = own_half(h)
        src, dst = ((SA, RA), (SB, RB), (SC, RC))[kind]
        return remote(src.at[row], dst.at[row], rs_s.at[h, kind], rs_r.at[h, kind], ypeer if kind == 1 else sib)

    def rs_first(h):
        SA[own_half(h), :] = PBUF[0:half, :].astype(bf16)
        rs_copy(h, 0).start()

    def rs_mid(h, term):
        rs_copy(h, 0).wait_recv()
        SB[own_half(h), :] = (term + RA[own_half(h), :].astype(f32)).astype(bf16)
        rs_copy(h, 1).start()

    def rs_second(h):
        SC[own_half(h), :] = PBUF[0:half, :].astype(bf16)
        rs_copy(h, 2).start()
        ACC[own_half(h), :] = PBUF[half:R, :]

    def rs_run(part, hooks={}):
        @pl.loop(0, 4)
        def _(step):
            h = step // 2
            for place, hook in hooks.items():
                pl.when(step == place)(hook)
            PBUF[...] = part(pair(step % 2, h))

            @pl.when(step % 2 == 0)
            def _():
                rs_first(h)
                ACC[own_half(h), :] = PBUF[half:R, :]

            @pl.when(step % 2 == 1)
            def _():
                rs_mid(h, ACC[own_half(h), :])
                rs_second(h)

    def rs_wait(h):
        rs_copy(h, 2).wait_recv()
        rs_copy(h, 1).wait_recv()

    def rs_sum(row):
        return ACC[row, :] + RB[row, :].astype(f32) + RC[row, :].astype(f32)

    def rs_end(h):
        for kind in range(3):
            rs_copy(h, kind).wait_send()

    def by_chunk(h, body):
        @pl.loop(0, half // CHUNK)
        def _(index):
            first = h * half + index * CHUNK
            body(pl.ds(pl.multiple_of(first, CHUNK), CHUNK), pl.ds(pl.multiple_of(t * R + first, CHUNK), CHUNK))

    def head_mask(h):
        lane = lax.broadcasted_iota(jnp.int32, (R, HC), 1)
        return (lane >= h * HD) & (lane < (h + 1) * HD)

    def gsrc(l, first):
        if l == 1:
            return W, 0, first
        if first >= spans["down"][0]:
            return ACT, 1, first - spans["down"][0]
        if first >= spans["up"][0]:
            return GP, 1, first - spans["up"][0]
        return NF2, 1, first

    def gref(l, g, aa, bb):
        first, width = groups[g]
        buf, slot, place = gsrc(l, first)
        return buf.at[slot, shard(aa, bb), pl.ds(place, width)]

    def gb(l, g, j, aa):
        first, width = groups[g]
        return remote(
            gref(l, g, aa, near(j)), BR.at[j - 1, aa, :, pl.ds(first, width)], gb_s.at[l, g, j, aa], gb_r.at[l, g, j, aa],
            dp_dev(a, near(j)),
        )

    def ga(l, g, k):
        first, width = groups[g]
        return remote(
            gref(l, g, far(k), b), AR.at[k - 1, :, pl.ds(first, width)], ga_s.at[l, g, k], ga_r.at[l, g, k], dp_dev(far(k), b)
        )

    def g_start(l, g):
        if l == 0:
            pl.semaphore_wait(cred_b.at[g], B - 1)

        def one(k):
            repeat(1, B, lambda j: gb(l, g, j, far(k)).start())

        repeat(1, A + 1, one)

    def g_piece(l, g, aa):
        first, width = groups[g]
        repeat(1, B, lambda j: gb(l, g, j, aa).wait_recv())
        total = gref(l, g, aa, b)[...].astype(f32)
        for j in range(1, B):
            total = total + BR[j - 1, aa, :, first : first + width].astype(f32)
        return total

    def g_far(l, g, k):
        piece = gref(l, g, far(k), b)
        piece[...] = g_piece(l, g, far(k)).astype(bf16)
        ga(l, g, k).start()

    def g_own(l, g):
        first, width = groups[g]
        OST[l, :, first : first + width] = g_piece(l, g, a)
        if l == 1:
            repeat(
                1, B,
                lambda j: pl.semaphore_signal(cred_b.at[g], inc=1, device_id=dp_dev(a, near(j)), device_id_type=MESH),
            )

    pieces = [(l, g, k) for l in (1, 0) for name in ("down", "up", "qkv", "out") for g in sets[name] for k in range(1, A + 1)]
    passed = {"count": 0}

    def g_upto(point):
        due = -(-SCHEDULE[point] * len(pieces) // 96)
        for l, g, k in pieces[passed["count"] : due]:
            if l == 0 and k == 1:
                pl.semaphore_wait(cred_a.at[g], A - 1)
            if k == A:
                g_own(l, g)
            else:
                g_far(l, g, k)
        passed["count"] = max(due, passed["count"])

    def g_out(l, name):
        first, width = spans[name]
        return [
            pltpu.make_async_copy(OST.at[l, :, pl.ds(place, wide)], dst.at[l], loc.at[l, at])
            for at, (dst, place, wide) in enumerate(
                ((gq, 0, HC), (gk, HC, HC), (gv, 2 * HC, HC), (go, 3 * HC, HC), (gu, 4 * HC, FC), (gd, 4 * HC + FC, FC))
            )
            if first <= place < first + width
        ]

    def g_final(l, name):
        for g in sets[name]:
            first, width = groups[g]

            def one(k):
                ga(l, g, k).wait_recv()
                OST[l, :, first : first + width] += AR[k - 1, :, first : first + width].astype(f32)

            repeat(1, A, one)
            if l == 1:
                repeat(
                    1, A,
                    lambda k: pl.semaphore_signal(cred_a.at[g], inc=1, device_id=dp_dev(far(k), b), device_id_type=MESH),
                )
        for copy in g_out(l, name):
            copy.start()

    def g_sent(l, g):
        repeat(1, A, lambda k: ga(l, g, k).wait_send())

        def one(k):
            repeat(1, B, lambda j: gb(l, g, j, far(k)).wait_send())

        repeat(1, A + 1, one)

    def weight_grad(l, name, left, right):
        first, width = spans[name]
        buf, slot, place = gsrc(l, first)

        @pl.loop(0, D // R)
        def _(i):
            buf[slot, blk(i), place : place + width] = dot_tn(left[:, blk(i)], right[...]).astype(bf16)

        for g in sets[name]:
            g_start(l, g)

    def reload(at):
        first, width = tuple(spans.values())[at]
        return pltpu.make_async_copy(spill.at[:, pl.ds(first, width)], W.at[1, :, pl.ds(first, width)], loc.at[1, 6 + at])

    def vgx(l, j):
        return remote(vg.at[l], VGX.at[l, j - 1], vgx_s.at[l, j], vgx_r.at[l, j], dp_dev(a, near(j)))

    def vgz(l, k):
        return remote(VGS.at[l], VGZ.at[l, k - 1], vgz_s.at[l, k], vgz_r.at[l, k], dp_dev(far(k), b))

    def vgt(l, i):
        return remote(VGU.at[l], VGT.at[l, i - 1], vgt_s.at[l, i], vgt_r.at[l, i], (dp, flip(i)))

    def vg_near(l):
        repeat(1, B, lambda j: vgx(l, j).start())

    def vg_far(l):
        repeat(1, B, lambda j: vgx(l, j).wait_recv())
        VGS[l] = vg[l]
        for j in range(1, B):
            VGS[l] += VGX[l, j - 1]
        repeat(1, A, lambda k: vgz(l, k).start())

    def vg_tensor(l):
        repeat(1, A, lambda k: vgz(l, k).wait_recv())
        VGU[l] = VGS[l]
        for k in range(1, A):
            VGU[l] += VGZ[l, k - 1]
        repeat(1, 4, lambda i: vgt(l, i).start())

    def own_lanes(ref, start):
        if S % 128 == 0:
            return ref[:, pl.ds(pl.multiple_of(start, 128), S)]
        tile = ref[:, pl.ds(pl.multiple_of(start // 128 * 128, 128), 128)]
        return pltpu.roll(tile, (128 - start % 128) % 128, 1)[:, 0:S]

    def vg_end(l):
        repeat(1, 4, lambda i: vgt(l, i).wait_recv())
        owner = dp // quarter
        total = VGU[l]
        picked = jnp.where(flip(0) == owner, VGU[l], 0.0)
        for i in range(1, 4):
            total = total + VGT[l, i - 1]
            picked = picked + jnp.where(flip(i) == owner, VGT[l, i - 1], 0.0)
        TOT[0:8, :] = total
        TOT[8:16, :] = picked
        inside = dp % quarter
        VS[l, 0:6, 0:S] = own_lanes(TOT.at[0:8], dp * S)[0:6, :]
        VS[l, 6:7, 0:S] = own_lanes(TOT.at[8:16], inside * S)[7:8, :]
        VS[l, 7:8, 0:S] = own_lanes(TOT.at[8:16], HC + inside * S)[7:8, :]
        for q in range(4):
            VS[l, 8 + q : 9 + q, 0:S] = own_lanes(TOT.at[8:16], inside * 4 * S + q * S)[6:7, :]
        repeat(1, B, lambda j: vgx(l, j).wait_send())
        repeat(1, A, lambda k: vgz(l, k).wait_send())
        repeat(1, 4, lambda i: vgt(l, i).wait_send())

    def low_grad(l, row, full, grad):
        GC[row, :] = grad
        low = grad.astype(bf16)
        GF[full, :] = low
        vg[l, 5:6, :] += jnp.sum(low.astype(f32), axis=0, keepdims=True)

    def pre_back(l, rows):
        act_grad = dot_nn(both(GF, rows), W[1, :, 4 * HC + FC : 4 * HC + 2 * FC])
        pre_grad = (act_grad * both(GP.at[l], rows).astype(f32)).astype(bf16)
        put(GP.at[l], rows, pre_grad)
        vg[l, 6:7, :] += jnp.sum(pre_grad.astype(f32), axis=0, keepdims=True)
        return pre_grad

    def norm_back(l, place, dy, rows, gain):
        n, scale = norm_parts(rows)
        vg[l, place : place + 1, :] += jnp.sum(dy * n, axis=0, keepdims=True)
        vg[l, place + 1 : place + 2, :] += jnp.sum(dy, axis=0, keepdims=True)
        dn = dy * gain
        return scale * (dn - jnp.mean(dn, axis=-1, keepdims=True) - n * jnp.mean(dn * n, axis=-1, keepdims=True))

    def vz(k, source, device):
        ref = RAW.at[source * B + b]
        return remote(ref, ref, vz_s.at[k], vz_r.at[k], device)

    def vx(k, j, minor, device):
        ref = RAW.at[(a - k + A) % A * B + minor]
        return remote(ref, ref, vx_s.at[k, j], vx_r.at[k, j], device)

    def v_send_x(k):
        repeat(1, B, lambda j: vx(k, j, b, dp_dev(a, near(j))).start())

    def v_pass(k):
        vz(k, (a - k + A) % A, dp_dev(far(k), b)).wait_recv()
        v_send_x(k)

    def v_done(k):
        repeat(1, B, lambda j: vx(k, j, (b - j + B) % B, dp_dev(a, near(j))).wait_recv())

    def v_sent(k):
        repeat(1, B, lambda j: vx(k, j, b, dp_dev(a, near(j))).wait_send())

    repeat(1, A, lambda k: vz(k, a, dp_dev(far(k), b)).start())
    v_send_x(0)

    w_wave()
    tok_copy.wait()
    repeat(1, A, v_pass)
    repeat(0, A, v_done)
    repeat(1, A, lambda k: vz(k, a, dp_dev(far(k), b)).wait_send())
    repeat(0, A, v_sent)

    def lay_out(row, offset, pieces):
        per_tile = max(1, 128 // S)
        for start in range(0, len(pieces), per_tile):
            run = pieces[start : start + per_tile]
            value = run[0] if len(run) == 1 else jnp.concatenate([piece[:, 0:S] for piece in run], axis=1)
            at = offset + start * S
            vec[row[0], row[1] : row[1] + 1, at : at + len(run) * S] = value[:, 0 : len(run) * S]

    for l in range(2):
        for place in range(6):
            lay_out((l, place), 0, [RAW[d, 12 * l + place : 12 * l + place + 1, :] for d in range(A * B)])
        for place in range(2):
            lay_out(
                (l, 7), place * HC,
                [RAW[t * quarter + d, 12 * l + 6 + place : 12 * l + 7 + place, :] for d in range(quarter)],
            )
        lay_out(
            (l, 6), 0,
            [RAW[t * quarter + d, 12 * l + 8 + q : 12 * l + 9 + q, :] for d in range(quarter) for q in range(4)],
        )

    spills = [
        pltpu.make_async_copy(W.at[0, :, pl.ds(first, width)], spill.at[:, pl.ds(first, width)], loc.at[1, 6 + at])
        for at, (first, width) in enumerate(spans.values())
    ]

    def first_norm(l, row, full):
        n, _ = norm_parts(X[l, row, :])
        NF[l, full, :] = (n * vec[l, 0:1, :] + vec[l, 1:2, :]).astype(bf16)

    @pl.loop(0, 2)
    def _(h):
        def one(row, full):
            X[0, row, :] = STB[row, :].astype(f32)
            first_norm(0, row, full)

        by_chunk(h, one)
        ag_start(NF.at[0], h)

    cot_copy.start()
    cot_copy.wait()

    @pl.loop(0, 2)
    def _(h):
        by_chunk(h, lambda row, full: low_grad(1, row, full, STB[row, :].astype(f32) * live))
        ag_start(GF, h, 1)

    for l in range(2):
        if l == 0:
            w_pass(0, "qkv")
        w_done(l, "qkv")
        w_pass(l, "out")

        def project(rows):
            out = dot_nn(both(NF.at[l], rows), W[l, :, 0 : 3 * HC])
            queries = out[:, 0:HC] + vec[l, 7:8, 0:HC]
            values = out[:, 2 * HC : 3 * HC] + vec[l, 7:8, HC : 2 * HC]
            put(QKV.at[l], rows, jnp.concatenate([queries, out[:, HC : 2 * HC], values], axis=1).astype(bf16))

        @pl.loop(0, 4)
        def _(step):
            h = step % 2
            pl.when(step < 2)(lambda: ag_near(NF.at[l], h))
            pl.when(step >= 2)(lambda: ag_far(NF.at[l], h))
            project(pair(1 - step // 2, h))

        if l == 0:

            @pl.loop(0, 2)
            def _(h):
                ag_near(GF, h, 1)
                ag_far(GF, h, 1)

        TR[...] = QKV[l, :, 2 * HC : 3 * HC].T
        w_done(l, "out")

        def attend(rows):
            queries = both(QKV.at[l, :, pl.ds(0, HC)], rows)
            keys = QKV[l, :, HC : 2 * HC]
            outs = []
            for h in range(heads):
                masked = jnp.where(head_mask(h), queries, jnp.zeros_like(queries))
                scores = dot_nt(keys, masked) * (score_scale * LOG2E)
                top = jnp.max(scores, axis=0, keepdims=True)
                exps = jnp.exp2(scores - top)
                total = jnp.sum(exps, axis=0, keepdims=True)
                log_sum = top + jnp.log(total) * LOG2E
                LSE[l, h : h + 1, rows[0]] = log_sum[:, 0:half]
                LSE[l, h : h + 1, rows[1]] = log_sum[:, half:R]
                outs.append(dot_nn(TR[h * HD : (h + 1) * HD, :], exps.astype(bf16)) * (1.0 / total))
            attended = jnp.concatenate(outs, axis=0).T.astype(bf16)
            put(AT.at[l], rows, attended)
            return dot_nt(attended, W[l, :, 3 * HC : 4 * HC])

        rs_run(
            attend,
            {1: lambda: w_pass(l, "up", 1), 2: lambda: w_pass(l, "up", 2), 3: lambda: w_pass(l, "up", 3)},
        )

        @pl.loop(0, 2)
        def _(h):
            pl.when(h == 1)(lambda: w_pass(l, "up"))
            rs_wait(h)

            def second_norm(row, full):
                middle = X[l, row, :] + rs_sum(row) + vec[l, 2:3, :]
                MID[l, row, :] = middle
                n, _ = norm_parts(middle)
                NF2[l, full, :] = (n * vec[l, 3:4, :] + vec[l, 4:5, :]).astype(bf16)

            by_chunk(h, second_norm)
            rs_end(h)
            ag_start(NF2.at[l], h)

        w_done(l, "up")

        @pl.loop(0, 4)
        def _(step):
            h = step % 2
            pl.when(step == 0)(lambda: w_pass(l, "down", 1))
            pl.when(step == 2)(lambda: w_pass(l, "down", 2))
            pl.when(step == 3)(lambda: w_pass(l, "down", 3))
            pl.when(step < 2)(lambda: ag_near(NF2.at[l], h))
            pl.when(step >= 2)(lambda: ag_far(NF2.at[l], h))
            rows = pair(1 - step // 2, h)
            pre = dot_nn(both(NF2.at[l], rows), W[l, :, 4 * HC : 4 * HC + FC]) + vec[l, 6:7, :]
            cumul = 0.5 * (1.0 + lax.erf(pre * ROOT_HALF))
            put(ACT.at[l], rows, (pre * cumul).astype(bf16))
            put(GP.at[l], rows, (cumul + pre * (jnp.exp(-0.5 * pre * pre) * PHI_ZERO)).astype(bf16))

        if l == 1:
            w_pass(1, "down", 3)
            for copy in spills:
                copy.wait()
            weight_grad(1, "down", GF, ACT.at[1])
        w_pass(l, "down")
        w_done(l, "down")

        def feed_out(rows):
            return dot_nt(both(ACT.at[l], rows), W[l, :, 4 * HC + FC : 4 * HC + 2 * FC])

        if l == 0:
            rs_run(feed_out, {2: lambda: w_pass(1, "qkv", 1, 3)})
            w_pass(1, "qkv", 2, 3)

            @pl.loop(0, 2)
            def _(h):
                pl.when(h == 1)(lambda: w_pass(1, "qkv"))
                rs_wait(h)

                def layer_out(row, full):
                    X[1, row, :] = MID[0, row, :] + rs_sum(row) + vec[0, 5:6, :]
                    first_norm(1, row, full)

                by_chunk(h, layer_out)
                rs_end(h)
                ag_start(NF.at[1], h)

        else:

            @pl.loop(0, 4)
            def _(step):
                pre_back(1, pair(step % 2, step // 2))

            rs_run(lambda rows: dot_nt(both(GP.at[1], rows), W[1, :, 4 * HC : 4 * HC + FC]))
            weight_grad(1, "up", NF2.at[1], GP.at[1])
            g_upto(0)

        if l == 0:
            for g in range(len(groups)):
                w_sent(0, g)
            for copy in spills:
                copy.start()

    def last_out(row, full):
        STB[row, :] = (MID[1, row, :] + rs_sum(row) + vec[1, 5:6, :]).astype(bf16)

    def greet_pairs():
        for device in (sib, ypeer):
            pl.semaphore_signal(ack, inc=1, device_id=device, device_id_type=MESH)
        pl.semaphore_wait(ack, 2)

    for l in (1, 0):
        if l == 0:
            reload(3).wait()
            reload(2).wait()

        if l == 0:

            def feed_back(rows):
                PBUF[...] = dot_nt(pre_back(0, rows), W[1, :, 4 * HC : 4 * HC + FC])

            @pl.loop(0, 2)
            def _(h):
                ag_near(GF, h)
                feed_back(near_pair(h))
                rs_second(h)

            g_upto(9)


            @pl.loop(0, 2)
            def _(h):
                @pl.when(h == 1)
                def _():
                    rs_mid(0, PBUF[half:R, :])
                    g_upto(10)

                ag_far(GF, h)
                feed_back(far_pair(h))
                rs_first(h)

            rs_mid(1, PBUF[half:R, :])
            g_upto(11)
            vg_far(1)
            g_final(1, "down")
            weight_grad(0, "down", GF, ACT.at[0])
            g_upto(12)

        @pl.loop(0, 2)
        def _(h):
            rs_wait(h)

            def second_back(row, full):
                grad = GC[row, :] + norm_back(l, 3, rs_sum(row), MID[l, row, :], vec[l, 3:4, :])
                GC[row, :] = grad
                low = grad.astype(bf16)
                MF[full, :] = low
                vg[l, 2:3, :] += jnp.sum(low.astype(f32), axis=0, keepdims=True)

            by_chunk(h, second_back)
            rs_end(h)
            ag_start(MF, h)

            @pl.when(h == 0)
            def _():
                if l == 0:
                    weight_grad(0, "up", NF2.at[0], GP.at[0])
                g_upto(2 if l == 1 else 13)

        if l == 0:
            vg_tensor(1)
            g_final(1, "up")
            g_upto(14)
            reload(1).wait()
            reload(0).wait()
        if l == 1:
            greet_pairs()
            rs_run(feed_out)
            g_upto(1)
        TR[...] = QKV[l, :, HC : 2 * HC].T
        DKA[...] = jnp.zeros_like(DKA)
        PBUF[...] = jnp.zeros_like(PBUF)

        @pl.loop(0, 4)
        def _(step):
            h = step % 2
            for place in (1, 2, 3):
                pl.when(step == place)(lambda: g_upto(place + (2 if l == 1 else 14)))
            pl.when(step < 2)(lambda: ag_near(MF, h))
            pl.when(step >= 2)(lambda: ag_far(MF, h))
            rows = pair(1 - step // 2, h)
            out_grads = dot_nn(both(MF, rows), W[1, :, 3 * HC : 4 * HC]).astype(bf16)
            queries = both(QKV.at[l, :, pl.ds(0, HC)], rows)
            keys = QKV[l, :, HC : 2 * HC]
            values = QKV[l, :, 2 * HC : 3 * HC]
            parts = []
            for head in range(heads):
                mask = head_mask(head)
                q_one = jnp.where(mask, queries, jnp.zeros_like(queries))
                do_one = jnp.where(mask, out_grads, jnp.zeros_like(out_grads))
                log_sum = jnp.concatenate([LSE[l, head : head + 1, rows[0]], LSE[l, head : head + 1, rows[1]]], axis=1)
                probs = jnp.exp2(dot_nt(keys, q_one) * (score_scale * LOG2E) - log_sum)
                prob_grad = dot_nt(values, do_one)
                value_part = dot_nn(probs.astype(bf16), do_one)
                for place in range(4):
                    PBUF[:, place * HC : (place + 1) * HC] += value_part[place * R : (place + 1) * R, :]
                row_dot = jnp.sum(probs * prob_grad, axis=0, keepdims=True)
                score_grad = (probs * (prob_grad - row_dot)).astype(bf16)
                DKA[...] += dot_nn(score_grad, q_one)
                parts.append(dot_nn(TR[head * HD : (head + 1) * HD, :], score_grad))
            query_low = (jnp.concatenate(parts, axis=0).T * score_scale).astype(bf16)
            put(DQKV.at[:, pl.ds(0, HC)], rows, query_low)

        g_upto(6 if l == 1 else 18)
        DQKV[:, HC : 2 * HC] = (DKA[...] * score_scale).astype(bf16)
        for place in range(4):
            DQKV[place * R : (place + 1) * R, 2 * HC : 3 * HC] = PBUF[:, place * HC : (place + 1) * HC].astype(bf16)
        weight_grad(l, "qkv", NF.at[l], DQKV)
        if l == 1:
            for g in range(len(groups)):
                w_sent(1, g)
            for at in (1, 2, 3):
                reload(at).start()

            @pl.loop(0, 2)
            def _(h):
                rs_wait(h)
                by_chunk(h, last_out)
                rs_end(h)

            mixed_copy = pltpu.make_async_copy(STB, mixed.at[0], loc.at[0, 6])
            mixed_copy.start()
            greet_pairs()
        g_upto(7 if l == 1 else 19)
        rs_run(lambda rows: dot_nt(both(DQKV, rows), W[1, :, 0 : 3 * HC]))
        if l == 1:
            reload(0).start()
        weight_grad(l, "out", MF, AT.at[l])
        vg[l, 7:8, 0:HC] = jnp.sum(DQKV[:, 0:HC].astype(f32), axis=0, keepdims=True)
        vg[l, 7:8, HC : 2 * HC] = jnp.sum(DQKV[:, 2 * HC : 3 * HC].astype(f32), axis=0, keepdims=True)
        g_upto(24 if l == 1 else 25)
        if l == 0:
            vg_end(1)

        @pl.loop(0, 2)
        def _(h):
            rs_wait(h)

            def first_back(row, full):
                grad = GC[row, :] + norm_back(l, 0, rs_sum(row), X[l, row, :], vec[l, 0:1, :])
                if l == 1:
                    low_grad(0, row, full, grad)
                else:
                    GC[row, :] = grad

            by_chunk(h, first_back)
            rs_end(h)
            if l == 1:
                ag_start(GF, h)

        vg_near(l)
        if l == 1:
            g_upto(8)

    mixed_copy.wait()
    grad_copy = pltpu.make_async_copy(GC, tgrad.at[0], loc.at[0, 7])
    grad_copy.start()
    g_upto(20)
    vg_far(0)
    g_final(1, "qkv")
    g_final(1, "out")
    g_upto(21)
    g_final(0, "down")
    vg_tensor(0)
    g_upto(22)
    vg_end(0)
    g_final(0, "up")
    g_upto(23)
    g_final(0, "qkv")
    vs_copy = pltpu.make_async_copy(VS, vs_out, loc.at[0, 6])
    vs_copy.start()
    g_final(0, "out")
    grad_copy.wait()
    vs_copy.wait()
    for l in range(2):
        for g in range(len(groups)):
            g_sent(l, g)
        for name in spans:
            for copy in g_out(l, name):
                copy.wait()


def finish_kernel(S, *refs):
    sources, small, targets, smalls, stages, sems = refs[:8], refs[8], refs[9:17], refs[17:26], refs[26:34], refs[34]
    arrivals = [
        pltpu.make_async_copy(source, stage, sems.at[0, at]) for at, (source, stage) in enumerate(zip(sources, stages))
    ]
    copies = [
        pltpu.make_async_copy(stage, target, sems.at[1, at]) for at, (stage, target) in enumerate(zip(stages, targets))
    ]
    for arrival in arrivals:
        arrival.start()
    for arrival, copy in zip(arrivals, copies):
        arrival.wait()
        copy.start()
    for l in range(2):
        for place in range(8):
            smalls[place][l : l + 1, :] = small[l, place : place + 1, 0:S]
        for q in range(4):
            smalls[8][l : l + 1, q * S : (q + 1) * S] = small[l, 8 + q : 9 + q, 0:S]
    for copy in copies:
        copy.wait()


def shards(
    mesh_dp,
    tokens, clip_counts, cotangent, norm1_gain, norm1_shift, w_query, query_bias, w_key, w_value, value_bias, w_out,
    out_bias, norm2_gain, norm2_shift, w_up, up_bias, w_down, down_bias,
):
    layers, S, HC = w_query.shape
    FC = w_up.shape[2]
    _, R, D = tokens.shape
    B = 1
    while 4 * B * B <= mesh_dp:
        B *= 2
    A = mesh_dp // B
    LEN = 4 * R
    COLS = 4 * HC + 2 * FC
    dims = (A, B, S, R, D, HC, FC)
    parts = COLS // HC if A * B <= 16 else 4
    vm = pltpu.VMEM
    dma = pltpu.SemaphoreType.DMA
    any_spec = pl.BlockSpec(memory_space=pl.ANY)
    vmem_spec = pl.BlockSpec(memory_space=pltpu.VMEM)
    grad_small = jax.ShapeDtypeStruct((layers, S, HC), f32)
    grad_large = jax.ShapeDtypeStruct((layers, S, FC), f32)
    outs = pl.pallas_call(
        functools.partial(encoder_kernel, dims),
        out_shape=(
            jax.ShapeDtypeStruct((1, R, D), bf16),
            jax.ShapeDtypeStruct((1, R, D), f32),
            grad_small, grad_small, grad_small, grad_small, grad_large, grad_large,
            jax.ShapeDtypeStruct((layers, 16, 128), f32),
            jax.ShapeDtypeStruct((D, COLS), bf16),
        ),
        in_specs=[any_spec, any_spec, pl.BlockSpec(memory_space=pltpu.SMEM)] + [any_spec] * 6 + [vmem_spec] * 9,
        out_specs=tuple([any_spec] * 10),
        scratch_shapes=[
            vm((2, D, COLS), bf16),
            vm((2, LEN, D), bf16),
            vm((2, LEN, 3 * HC), bf16),
            vm((2, LEN, HC), bf16),
            vm((2, 8, LEN), f32),
            vm((2, R, D), f32),
            vm((2, R, D), f32),
            vm((2, LEN, D), bf16),
            vm((2, LEN, FC), bf16),
            vm((2, LEN, FC), bf16),
            vm((LEN, D), bf16),
            vm((LEN, D), bf16),
            vm((LEN, 3 * HC), bf16),
            vm((R, D), f32),
            vm((max(B - 1, 1), A, S, COLS), bf16),
            vm((max(A - 1, 1), S, COLS), bf16),
            vm((R, D), bf16), vm((R, D), bf16), vm((R, D), bf16),
            vm((R, D), bf16), vm((R, D), bf16), vm((R, D), bf16),
            vm((R, D), f32), vm((R, D), f32),
            vm((2, S, COLS), f32),
            vm((HC, LEN), bf16),
            vm((LEN, HC), f32),
            vm((R, D), bf16),
            vm((A * B, 24, 128), f32),
            vm((2, 8, D), f32), vm((2, 8, D), f32),
            vm((2, max(B - 1, 1), 8, D), f32),
            vm((2, 8, D), f32),
            vm((2, max(A - 1, 1), 8, D), f32),
            vm((2, 8, D), f32),
            vm((2, 3, 8, D), f32),
            vm((2, 16, 128), f32),
            vm((16, D), f32),
            dma((2, 10)),
            dma((2, 2, 3)), dma((2, 2, 3)), dma((2, 3)), dma((2, 3)),
            dma((2 * parts, 2, A)), dma((2 * parts, 2, A)), dma((2 * parts, A, B)), dma((2 * parts, A, B)),
            dma((2, parts, B, A)), dma((2, parts, B, A)), dma((2, parts, A)), dma((2, parts, A)),
            dma((A,)), dma((A,)), dma((A, B)), dma((A, B)),
            dma((2, B)), dma((2, B)), dma((2, A)), dma((2, A)), dma((2, 4)), dma((2, 4)),
            pltpu.SemaphoreType.REGULAR((parts,)), pltpu.SemaphoreType.REGULAR((parts,)), pltpu.SemaphoreType.REGULAR,
        ],
        compiler_params=pltpu.CompilerParams(
            collective_id=0, has_side_effects=True, vmem_limit_bytes=64 * 2**20 - 2**17
        ),
        name="encoder",
    )(tokens, cotangent, clip_counts, w_query, w_key, w_value, w_out, w_up, w_down, norm1_gain, norm1_shift,
      out_bias, norm2_gain, norm2_shift, down_bias, query_bias, value_bias, up_bias)

    small = jax.ShapeDtypeStruct((layers, S), f32)
    large_types = tuple(jax.ShapeDtypeStruct(member.shape, member.dtype) for member in outs[:8])
    (mixed, tokens_grad, gq, gk, gv, go, gu, gd, g_gain_one, g_shift_one, g_out, g_gain_two, g_shift_two, g_down, g_query,
     g_value, g_up) = pl.pallas_call(
        functools.partial(finish_kernel, S),
        out_shape=large_types + (small,) * 8 + (jax.ShapeDtypeStruct((layers, 4 * S), f32),),
        in_specs=[any_spec] * 8 + [vmem_spec],
        out_specs=tuple([any_spec] * 8 + [vmem_spec] * 9),
        scratch_shapes=[vm(member.shape, member.dtype) for member in outs[:8]] + [dma((2, 8))],
        compiler_params=pltpu.CompilerParams(vmem_limit_bytes=64 * 2**20 - 2**17),
        name="finish",
    )(*outs[:9])
    return (
        mixed, tokens_grad, g_gain_one, g_shift_one, gq, g_query, gk, gv, g_value, go, g_out, g_gain_two, g_shift_two, gu,
        g_up, gd, g_down,
    )


def solution(mesh):
    rows = P("dp", "tensor", None)
    vector = P(None, "dp")
    matrix = P(None, "dp", "tensor")
    return jax.shard_map(
        functools.partial(shards, mesh.shape["dp"]),
        mesh=mesh,
        in_specs=(
            rows, P("dp"), rows, vector, vector, matrix, vector, matrix, matrix, vector, matrix, vector, vector, vector,
            matrix, vector, matrix, vector,
        ),
        out_specs=(
            rows, rows, vector, vector, matrix, vector, matrix, matrix, vector, matrix, vector, vector, vector, matrix,
            vector, matrix, vector,
        ),
        check_vma=False,
    )
```

```python
import functools
import math

import jax
import jax.numpy as jnp
from jax import lax
from jax.experimental import pallas as pl
from jax.experimental.pallas import tpu as pltpu
from jax.sharding import PartitionSpec as P

HD = 64
norm_eps = 1e-06
MESH = pl.DeviceIdType.MESH
bf16 = jnp.bfloat16
f32 = jnp.float32
ROOT_HALF = 1.0 / math.sqrt(2.0)
PHI_ZERO = 1.0 / math.sqrt(2.0 * math.pi)
LOG2E = 1.0 / math.log(2.0)
CHUNK = 64
SCHEDULE = (4, 18, 10, 22, 26, 30, 32, 32, 44, 48, 48, 48, 48, 56, 60, 64, 64, 68, 72, 76, 80, 88, 96, 96, 40, 80, 14)


def dot_nn(left, right):
    return jnp.dot(left, right, preferred_element_type=f32)


def dot_nt(left, right):
    return lax.dot_general(left, right, (((1,), (1,)), ((), ())), preferred_element_type=f32)


def dot_tn(left, right):
    return lax.dot_general(left, right, (((0,), (0,)), ((), ())), preferred_element_type=f32)


def repeat(low, high, body):
    if high - low <= 4:
        for index in range(low, high):
            body(index)
    else:

        pl.loop(low, high)(body)


def norm_parts(rows):
    centered = rows - jnp.mean(rows, axis=-1, keepdims=True)
    scale = lax.rsqrt(jnp.mean(centered * centered, axis=-1, keepdims=True) + norm_eps)
    return centered * scale, scale


def encoder_kernel(
    dims,
    tok, cot, counts, wq, wk, wv, wo, wu, wd, gain_one, shift_one, out_b, gain_two, shift_two, down_b, query_b, value_b, up_b,
    mixed, tgrad, gq, gk, gv, go, gu, gd, vs_out, spill,
    W, NF, QKV, AT, LSE, X, MID, NF2, ACT, GP, GF, MF, DQKV, GC, BR, AR,
    SA, SB, SC, RA, RB, RC, ACC, PBUF, OST, TR, DKA, STB, RAW, vec, vg, VGX, VGS, VGZ, VGU, VGT, VS, TOT,
    loc, ag_s, ag_r, rs_s, rs_r, wz_s, wz_r, wx_s, wx_r, gb_s, gb_r, ga_s, ga_r,
    vz_s, vz_r, vx_s, vx_r, vgx_s, vgx_r, vgz_s, vgz_r, vgt_s, vgt_r, cred_b, cred_a, ack,
):
    A, B, S, R, D, HC, FC = dims
    heads = HC // HD
    score_scale = HD ** (-0.5)
    dp = lax.axis_index("dp")
    t = lax.axis_index("tensor")
    a = dp // B
    b = dp % B
    y = t // 2
    c = t % 2

    def flip(i):
        return 2 * ((y + i // 2) % 2) + (c + i % 2) % 2

    sib = (dp, flip(1))
    ypeer = (dp, flip(2))
    corner = (dp, flip(3))

    def dp_dev(aa, bb):
        return (aa * B + bb, t)

    def far(k):
        return (a + k) % A

    def near(j):
        return (b + j) % B

    fine = A * B <= 16
    spans = {"qkv": (0, 3 * HC), "out": (3 * HC, HC), "up": (4 * HC, FC), "down": (4 * HC + FC, FC)}
    groups, sets = [], {}
    for name, (first, width) in spans.items():
        step = HC if fine else width
        sets[name] = tuple(range(len(groups), len(groups) + width // step))
        groups.extend((at, step) for at in range(first, first + width, step))

    def part(pieces, low, high, parts):
        return pieces[low * len(pieces) // parts : high * len(pieces) // parts]

    half = R // 2
    quarter = A * B // 4

    def own_half(h):
        return pl.ds(pl.multiple_of(h * half, half), half)

    def hrow(i, h):
        return pl.ds(pl.multiple_of(i * R + h * half, half), half)

    def near_pair(h):
        return hrow(flip(1), h), hrow(flip(0), h)

    def far_pair(h):
        return hrow(flip(3), h), hrow(flip(2), h)

    def pair(near, h):
        return hrow(flip(3 - 2 * near), h), hrow(flip(2 - 2 * near), h)

    def both(ref, rows):
        return jnp.concatenate([ref[rows[0], :], ref[rows[1], :]], axis=0)

    def put(ref, rows, value):
        ref[rows[0], :] = value[0:half]
        ref[rows[1], :] = value[half : 2 * half]

    def blk(i):
        return pl.ds(pl.multiple_of(i * R, R), R)

    def shard(aa, bb):
        return pl.ds(pl.multiple_of((aa * B + bb) * S, S), S)

    def remote(src, dst, send, recv, device):
        return pltpu.make_async_remote_copy(
            src_ref=src, dst_ref=dst, send_sem=send, recv_sem=recv, device_id=device, device_id_type=MESH
        )

    barrier = pltpu.get_barrier_semaphore()

    def greet(device):
        pl.semaphore_signal(barrier, inc=1, device_id=device, device_id_type=MESH)

    greet(sib)
    greet(ypeer)
    greet(corner)
    repeat(1, A, lambda k: greet(dp_dev(far(k), b)))
    repeat(1, B, lambda j: greet(dp_dev(a, near(j))))

    weights = (
        (wq, 0, HC), (wk, HC, HC), (wv, 2 * HC, HC), (wo, 3 * HC, HC), (wu, 4 * HC, FC), (wd, 4 * HC + FC, FC),
    )
    loads = {
        (l, at): pltpu.make_async_copy(src.at[l], W.at[l, shard(a, b), pl.ds(first, width)], loc.at[l, at])
        for l in range(2)
        for at, (src, first, width) in enumerate(weights)
    }
    for copy in loads.values():
        copy.start()
    tok_copy = pltpu.make_async_copy(tok.at[0], STB, loc.at[0, 6])
    tok_copy.start()
    cot_copy = pltpu.make_async_copy(cot.at[0], STB, loc.at[0, 7])
    live = counts[0].astype(f32)
    vg[...] = jnp.zeros_like(vg)
    vectors = (gain_one, shift_one, out_b, gain_two, shift_two, down_b, query_b, value_b)
    for l in range(2):
        for place, vector in enumerate(vectors):
            RAW[dp, 12 * l + place : 12 * l + place + 1, 0:S] = vector[...].astype(f32)[l : l + 1, :]
        for q in range(4):
            RAW[dp, 12 * l + 8 + q : 12 * l + 9 + q, 0:S] = up_b[...].astype(f32)[l : l + 1, q * S : (q + 1) * S]
    pl.semaphore_wait(barrier, A + B + 1)

    order = [(l, g) for l in range(2) for g in range(len(groups))]

    def wrow(n, source, minor):
        l, g = order[n]
        return W.at[l, shard(source, minor), pl.ds(groups[g][0], groups[g][1])]

    def wz(n, way, hop, source):
        ref = wrow(n, source, b)
        return remote(ref, ref, wz_s.at[n, way, hop], wz_r.at[n, way, hop], dp_dev(a + 1 - 2 * way, b))

    def wx(n, behind, j, minor):
        ref = wrow(n, (a - behind + A) % A, minor)
        return remote(ref, ref, wx_s.at[n, behind, j], wx_r.at[n, behind, j], dp_dev(a, near(j)))

    def w_send_x(n, behind):
        repeat(1, B, lambda j: wx(n, behind, j, b).start())

    def w_arrive(n, hop):
        @pl.when(a >= hop)
        def _():
            wz(n, 0, hop, a - hop).wait_recv()
            if hop < A - 1:
                pl.when(a < A - 1)(lambda: wz(n, 0, hop + 1, a - hop).start())
            w_send_x(n, hop)

        @pl.when(a + hop < A)
        def _():
            wz(n, 1, hop, a + hop).wait_recv()
            if hop < A - 1:
                pl.when(a > 0)(lambda: wz(n, 1, hop + 1, a + hop).start())
            w_send_x(n, A - hop)

    progress = {"wave": 0, "line": 0, "own": 0, "load": 0}

    def w_wave():
        wave = progress["wave"]
        for n in range(progress["line"], min(wave + 3, len(order))):
            l, g = order[n]
            first = groups[g][0]
            for at, (_, place, wide) in enumerate(weights):
                if first <= place < first + groups[g][1]:
                    loads[l, at].wait()
            pl.when(a < A - 1)(lambda: wz(n, 0, 1, a).start())
            pl.when(a > 0)(lambda: wz(n, 1, 1, a).start())
            progress["line"] = n + 1
        for n in range(progress["own"], min(wave + 6, progress["line"] + 3, len(order))):
            if n < progress["line"]:
                w_send_x(n, 0)
                progress["own"] = n + 1
        for hop in range(1, A):
            if 0 <= wave - hop + 1 < len(order):
                w_arrive(wave - hop + 1, hop)
        progress["wave"] = wave + 1

    def w_pass(l, name, count=4, parts=4):
        chosen = part(sets[name], 0, count, parts)
        if chosen:
            while progress["wave"] < order.index((l, chosen[-1])) + A - 1:
                w_wave()

    def w_done(l, name):
        def one(n, behind):
            repeat(1, B, lambda j: wx(n, behind, j, (b - j + B) % B).wait_recv())

        for g in sets[name]:
            repeat(0, A, functools.partial(one, order.index((l, g))))

    def w_sent(l, g):
        n = order.index((l, g))
        pl.when(a < A - 1)(lambda: wz(n, 0, 1, a).wait_send())
        pl.when(a > 0)(lambda: wz(n, 1, 1, a).wait_send())
        for hop in range(1, A - 1):
            pl.when((a >= hop) & (a < A - 1))(lambda: wz(n, 0, hop + 1, a - hop).wait_send())
            pl.when((a + hop < A) & (a > 0))(lambda: wz(n, 1, hop + 1, a + hop).wait_send())

        def one(behind):
            repeat(1, B, lambda j: wx(n, behind, j, b).wait_send())

        repeat(0, A, one)

    def ag_copy(buf, h, kind, early=0):
        row = hrow(flip(2), h) if kind == 2 else hrow(t, h)
        send, recv = ag_s.at[early, h, kind], ag_r.at[early, h, kind]
        return remote(buf.at[row], buf.at[row], send, recv, ypeer if kind == 0 else sib)

    def ag_arrival(buf, h, kind, early=0):
        row = hrow(flip((2, 1, 3)[kind]), h)
        send, recv = ag_s.at[early, h, kind], ag_r.at[early, h, kind]
        return remote(buf.at[row], buf.at[row], send, recv, ypeer if kind == 0 else sib)

    def ag_start(buf, h, early=0):
        ag_copy(buf, h, 0, early).start()
        ag_copy(buf, h, 1, early).start()

    def ag_near(buf, h, early=0):
        ag_arrival(buf, h, 1, early).wait_recv()

    def ag_far(buf, h, early=0):
        ag_arrival(buf, h, 0, early).wait_recv()
        ag_copy(buf, h, 2, early).start()
        ag_arrival(buf, h, 2, early).wait_recv()
        for kind in range(3):
            ag_copy(buf, h, kind, early).wait_send()

    def rs_copy(h, kind):
        row = own_half(h)
        src, dst = ((SA, RA), (SB, RB), (SC, RC))[kind]
        return remote(src.at[row], dst.at[row], rs_s.at[h, kind], rs_r.at[h, kind], ypeer if kind == 1 else sib)

    def rs_first(h):
        SA[own_half(h), :] = PBUF[0:half, :].astype(bf16)
        rs_copy(h, 0).start()

    def rs_mid(h, term):
        rs_copy(h, 0).wait_recv()
        SB[own_half(h), :] = (term + RA[own_half(h), :].astype(f32)).astype(bf16)
        rs_copy(h, 1).start()

    def rs_second(h):
        SC[own_half(h), :] = PBUF[0:half, :].astype(bf16)
        rs_copy(h, 2).start()
        ACC[own_half(h), :] = PBUF[half:R, :]

    def rs_run(part, hooks={}):
        @pl.loop(0, 4)
        def _(step):
            h = step // 2
            for place, hook in hooks.items():
                pl.when(step == place)(hook)
            PBUF[...] = part(pair(step % 2, h))

            @pl.when(step % 2 == 0)
            def _():
                rs_first(h)
                ACC[own_half(h), :] = PBUF[half:R, :]

            @pl.when(step % 2 == 1)
            def _():
                rs_mid(h, ACC[own_half(h), :])
                rs_second(h)

    def rs_wait(h):
        rs_copy(h, 2).wait_recv()
        rs_copy(h, 1).wait_recv()

    def rs_sum(row):
        return ACC[row, :] + RB[row, :].astype(f32) + RC[row, :].astype(f32)

    def rs_end(h):
        for kind in range(3):
            rs_copy(h, kind).wait_send()

    def by_chunk(h, body):
        @pl.loop(0, half // CHUNK)
        def _(index):
            first = h * half + index * CHUNK
            body(pl.ds(pl.multiple_of(first, CHUNK), CHUNK), pl.ds(pl.multiple_of(t * R + first, CHUNK), CHUNK))

    def head_mask(h):
        lane = lax.broadcasted_iota(jnp.int32, (R, HC), 1)
        return (lane >= h * HD) & (lane < (h + 1) * HD)

    def gsrc(l, first):
        if l == 1:
            return W, 0, first
        if first >= spans["down"][0]:
            return ACT, 1, first - spans["down"][0]
        if first >= spans["up"][0]:
            return GP, 1, first - spans["up"][0]
        return NF2, 1, first

    def gref(l, g, aa, bb):
        first, width = groups[g]
        buf, slot, place = gsrc(l, first)
        return buf.at[slot, shard(aa, bb), pl.ds(place, width)]

    def gb(l, g, j, aa):
        first, width = groups[g]
        return remote(
            gref(l, g, aa, near(j)), BR.at[j - 1, aa, :, pl.ds(first, width)], gb_s.at[l, g, j, aa], gb_r.at[l, g, j, aa],
            dp_dev(a, near(j)),
        )

    def ga(l, g, k):
        first, width = groups[g]
        return remote(
            gref(l, g, far(k), b), AR.at[k - 1, :, pl.ds(first, width)], ga_s.at[l, g, k], ga_r.at[l, g, k], dp_dev(far(k), b)
        )

    def g_start(l, g):
        if l == 0:
            pl.semaphore_wait(cred_b.at[g], B - 1)

        def one(k):
            repeat(1, B, lambda j: gb(l, g, j, far(k)).start())

        repeat(1, A + 1, one)

    def g_piece(l, g, aa):
        first, width = groups[g]
        repeat(1, B, lambda j: gb(l, g, j, aa).wait_recv())
        total = gref(l, g, aa, b)[...].astype(f32)
        for j in range(1, B):
            total = total + BR[j - 1, aa, :, first : first + width].astype(f32)
        return total

    def g_far(l, g, k):
        piece = gref(l, g, far(k), b)
        piece[...] = g_piece(l, g, far(k)).astype(bf16)
        ga(l, g, k).start()

    def g_own(l, g):
        first, width = groups[g]
        OST[l, :, first : first + width] = g_piece(l, g, a)
        if l == 1:
            repeat(
                1, B,
                lambda j: pl.semaphore_signal(cred_b.at[g], inc=1, device_id=dp_dev(a, near(j)), device_id_type=MESH),
            )

    pieces = [(l, g, k) for l in (1, 0) for name in ("down", "up", "qkv", "out") for g in sets[name] for k in range(1, A + 1)]
    passed = {"count": 0}

    def g_upto(point):
        left, due = SCHEDULE[point], 0
        for name, size in 2 * (("down", 16), ("up", 16), ("qkv", 12), ("out", 4)):
            due += min(left, size) * len(sets[name]) * A // size
            left = max(left - size, 0)
        for l, g, k in pieces[passed["count"] : due]:
            if l == 0 and k == 1:
                pl.semaphore_wait(cred_a.at[g], A - 1)
            if k == A:
                g_own(l, g)
            else:
                g_far(l, g, k)
        passed["count"] = max(due, passed["count"])

    def g_out(l, name):
        first, width = spans[name]
        return [
            pltpu.make_async_copy(OST.at[l, :, pl.ds(place, wide)], dst.at[l], loc.at[l, at])
            for at, (dst, place, wide) in enumerate(
                ((gq, 0, HC), (gk, HC, HC), (gv, 2 * HC, HC), (go, 3 * HC, HC), (gu, 4 * HC, FC), (gd, 4 * HC + FC, FC))
            )
            if first <= place < first + width
        ]

    def g_final(l, name):
        for g in sets[name]:
            first, width = groups[g]

            def one(k):
                ga(l, g, k).wait_recv()
                OST[l, :, first : first + width] += AR[k - 1, :, first : first + width].astype(f32)

            repeat(1, A, one)
            if l == 1:
                repeat(
                    1, A,
                    lambda k: pl.semaphore_signal(cred_a.at[g], inc=1, device_id=dp_dev(far(k), b), device_id_type=MESH),
                )
        for copy in g_out(l, name):
            copy.start()

    def g_sent(l, g):
        repeat(1, A, lambda k: ga(l, g, k).wait_send())

        def one(k):
            repeat(1, B, lambda j: gb(l, g, j, far(k)).wait_send())

        repeat(1, A + 1, one)

    def weight_grad(l, name, left, right):
        first, width = spans[name]
        buf, slot, place = gsrc(l, first)

        @pl.loop(0, D // R)
        def _(i):
            buf[slot, blk(i), place : place + width] = dot_tn(left[:, blk(i)], right[...]).astype(bf16)

        for g in sets[name]:
            g_start(l, g)

    def reload(at):
        first, width = tuple(spans.values())[at]
        return pltpu.make_async_copy(spill.at[:, pl.ds(first, width)], W.at[1, :, pl.ds(first, width)], loc.at[1, 6 + at])

    def vgx(l, j):
        return remote(vg.at[l], VGX.at[l, j - 1], vgx_s.at[l, j], vgx_r.at[l, j], dp_dev(a, near(j)))

    def vgz(l, k):
        return remote(VGS.at[l], VGZ.at[l, k - 1], vgz_s.at[l, k], vgz_r.at[l, k], dp_dev(far(k), b))

    def vgt(l, i):
        return remote(VGU.at[l], VGT.at[l, i - 1], vgt_s.at[l, i], vgt_r.at[l, i], (dp, flip(i)))

    def vg_near(l):
        repeat(1, B, lambda j: vgx(l, j).start())

    def vg_far(l):
        repeat(1, B, lambda j: vgx(l, j).wait_recv())
        VGS[l] = vg[l]
        for j in range(1, B):
            VGS[l] += VGX[l, j - 1]
        repeat(1, A, lambda k: vgz(l, k).start())

    def vg_tensor(l):
        repeat(1, A, lambda k: vgz(l, k).wait_recv())
        VGU[l] = VGS[l]
        for k in range(1, A):
            VGU[l] += VGZ[l, k - 1]
        repeat(1, 4, lambda i: vgt(l, i).start())

    def own_lanes(ref, start):
        if S % 128 == 0:
            return ref[:, pl.ds(pl.multiple_of(start, 128), S)]
        tile = ref[:, pl.ds(pl.multiple_of(start // 128 * 128, 128), 128)]
        return pltpu.roll(tile, (128 - start % 128) % 128, 1)[:, 0:S]

    def vg_end(l):
        repeat(1, 4, lambda i: vgt(l, i).wait_recv())
        owner = dp // quarter
        total = VGU[l]
        picked = jnp.where(flip(0) == owner, VGU[l], 0.0)
        for i in range(1, 4):
            total = total + VGT[l, i - 1]
            picked = picked + jnp.where(flip(i) == owner, VGT[l, i - 1], 0.0)
        TOT[0:8, :] = total
        TOT[8:16, :] = picked
        inside = dp % quarter
        VS[l, 0:6, 0:S] = own_lanes(TOT.at[0:8], dp * S)[0:6, :]
        VS[l, 6:7, 0:S] = own_lanes(TOT.at[8:16], inside * S)[7:8, :]
        VS[l, 7:8, 0:S] = own_lanes(TOT.at[8:16], HC + inside * S)[7:8, :]
        for q in range(4):
            VS[l, 8 + q : 9 + q, 0:S] = own_lanes(TOT.at[8:16], inside * 4 * S + q * S)[6:7, :]
        repeat(1, B, lambda j: vgx(l, j).wait_send())
        repeat(1, A, lambda k: vgz(l, k).wait_send())
        repeat(1, 4, lambda i: vgt(l, i).wait_send())

    def low_grad(l, row, full, grad):
        GC[row, :] = grad
        low = grad.astype(bf16)
        GF[full, :] = low
        vg[l, 5:6, :] += jnp.sum(low.astype(f32), axis=0, keepdims=True)

    def pre_back(l, rows):
        act_grad = dot_nn(both(GF, rows), W[1, :, 4 * HC + FC : 4 * HC + 2 * FC])
        pre_grad = (act_grad * both(GP.at[l], rows).astype(f32)).astype(bf16)
        put(GP.at[l], rows, pre_grad)
        vg[l, 6:7, :] += jnp.sum(pre_grad.astype(f32), axis=0, keepdims=True)
        return pre_grad

    def norm_back(l, place, dy, rows, gain):
        n, scale = norm_parts(rows)
        vg[l, place : place + 1, :] += jnp.sum(dy * n, axis=0, keepdims=True)
        vg[l, place + 1 : place + 2, :] += jnp.sum(dy, axis=0, keepdims=True)
        dn = dy * gain
        return scale * (dn - jnp.mean(dn, axis=-1, keepdims=True) - n * jnp.mean(dn * n, axis=-1, keepdims=True))

    def vz(k, source, device):
        ref = RAW.at[source * B + b]
        return remote(ref, ref, vz_s.at[k], vz_r.at[k], device)

    def vx(k, j, minor, device):
        ref = RAW.at[(a - k + A) % A * B + minor]
        return remote(ref, ref, vx_s.at[k, j], vx_r.at[k, j], device)

    def v_send_x(k):
        repeat(1, B, lambda j: vx(k, j, b, dp_dev(a, near(j))).start())

    def v_pass(k):
        vz(k, (a - k + A) % A, dp_dev(far(k), b)).wait_recv()
        v_send_x(k)

    def v_done(k):
        repeat(1, B, lambda j: vx(k, j, (b - j + B) % B, dp_dev(a, near(j))).wait_recv())

    def v_sent(k):
        repeat(1, B, lambda j: vx(k, j, b, dp_dev(a, near(j))).wait_send())

    repeat(1, A, lambda k: vz(k, a, dp_dev(far(k), b)).start())
    v_send_x(0)

    w_wave()
    tok_copy.wait()
    repeat(1, A, v_pass)
    repeat(0, A, v_done)
    repeat(1, A, lambda k: vz(k, a, dp_dev(far(k), b)).wait_send())
    repeat(0, A, v_sent)

    def lay_out(row, offset, pieces):
        per_tile = max(1, 128 // S)
        for start in range(0, len(pieces), per_tile):
            run = pieces[start : start + per_tile]
            value = run[0] if len(run) == 1 else jnp.concatenate([piece[:, 0:S] for piece in run], axis=1)
            at = offset + start * S
            vec[row[0], row[1] : row[1] + 1, at : at + len(run) * S] = value[:, 0 : len(run) * S]

    for l in range(2):
        for place in range(6):
            lay_out((l, place), 0, [RAW[d, 12 * l + place : 12 * l + place + 1, :] for d in range(A * B)])
        for place in range(2):
            lay_out(
                (l, 7), place * HC,
                [RAW[t * quarter + d, 12 * l + 6 + place : 12 * l + 7 + place, :] for d in range(quarter)],
            )
        lay_out(
            (l, 6), 0,
            [RAW[t * quarter + d, 12 * l + 8 + q : 12 * l + 9 + q, :] for d in range(quarter) for q in range(4)],
        )

    spills = [
        pltpu.make_async_copy(W.at[0, :, pl.ds(first, width)], spill.at[:, pl.ds(first, width)], loc.at[1, 6 + at])
        for at, (first, width) in enumerate(spans.values())
    ]

    def first_norm(l, row, full):
        n, _ = norm_parts(X[l, row, :])
        NF[l, full, :] = (n * vec[l, 0:1, :] + vec[l, 1:2, :]).astype(bf16)

    @pl.loop(0, 2)
    def _(h):
        def one(row, full):
            X[0, row, :] = STB[row, :].astype(f32)
            first_norm(0, row, full)

        by_chunk(h, one)
        ag_start(NF.at[0], h)

    cot_copy.start()
    cot_copy.wait()

    @pl.loop(0, 2)
    def _(h):
        by_chunk(h, lambda row, full: low_grad(1, row, full, STB[row, :].astype(f32) * live))
        ag_start(GF, h, 1)

    for l in range(2):
        if l == 0:
            w_pass(0, "qkv")
        w_done(l, "qkv")
        w_pass(l, "out")

        def project(rows):
            out = dot_nn(both(NF.at[l], rows), W[l, :, 0 : 3 * HC])
            queries = out[:, 0:HC] + vec[l, 7:8, 0:HC]
            values = out[:, 2 * HC : 3 * HC] + vec[l, 7:8, HC : 2 * HC]
            put(QKV.at[l], rows, jnp.concatenate([queries, out[:, HC : 2 * HC], values], axis=1).astype(bf16))

        @pl.loop(0, 4)
        def _(step):
            h = step % 2
            pl.when(step < 2)(lambda: ag_near(NF.at[l], h))
            pl.when(step >= 2)(lambda: ag_far(NF.at[l], h))
            project(pair(1 - step // 2, h))

        if l == 0:

            @pl.loop(0, 2)
            def _(h):
                ag_near(GF, h, 1)
                ag_far(GF, h, 1)

        TR[...] = QKV[l, :, 2 * HC : 3 * HC].T
        w_done(l, "out")

        def attend(rows):
            queries = both(QKV.at[l, :, pl.ds(0, HC)], rows)
            keys = QKV[l, :, HC : 2 * HC]
            outs = []
            for h in range(heads):
                masked = jnp.where(head_mask(h), queries, jnp.zeros_like(queries))
                scores = dot_nt(keys, masked) * (score_scale * LOG2E)
                top = jnp.max(scores, axis=0, keepdims=True)
                exps = jnp.exp2(scores - top)
                total = jnp.sum(exps, axis=0, keepdims=True)
                log_sum = top + jnp.log(total) * LOG2E
                LSE[l, h : h + 1, rows[0]] = log_sum[:, 0:half]
                LSE[l, h : h + 1, rows[1]] = log_sum[:, half:R]
                outs.append(dot_nn(TR[h * HD : (h + 1) * HD, :], exps.astype(bf16)) * (1.0 / total))
            attended = jnp.concatenate(outs, axis=0).T.astype(bf16)
            put(AT.at[l], rows, attended)
            return dot_nt(attended, W[l, :, 3 * HC : 4 * HC])

        rs_run(
            attend,
            {1: lambda: w_pass(l, "up", 1), 2: lambda: w_pass(l, "up", 2), 3: lambda: w_pass(l, "up", 3)},
        )

        @pl.loop(0, 2)
        def _(h):
            pl.when(h == 1)(lambda: w_pass(l, "up"))
            rs_wait(h)

            def second_norm(row, full):
                middle = X[l, row, :] + rs_sum(row) + vec[l, 2:3, :]
                MID[l, row, :] = middle
                n, _ = norm_parts(middle)
                NF2[l, full, :] = (n * vec[l, 3:4, :] + vec[l, 4:5, :]).astype(bf16)

            by_chunk(h, second_norm)
            rs_end(h)
            ag_start(NF2.at[l], h)

        w_done(l, "up")

        @pl.loop(0, 4)
        def _(step):
            h = step % 2
            pl.when(step == 0)(lambda: w_pass(l, "down", 1))
            pl.when(step == 2)(lambda: w_pass(l, "down", 2))
            pl.when(step == 3)(lambda: w_pass(l, "down", 3))
            pl.when(step < 2)(lambda: ag_near(NF2.at[l], h))
            pl.when(step >= 2)(lambda: ag_far(NF2.at[l], h))
            rows = pair(1 - step // 2, h)
            pre = dot_nn(both(NF2.at[l], rows), W[l, :, 4 * HC : 4 * HC + FC]) + vec[l, 6:7, :]
            cumul = 0.5 * (1.0 + lax.erf(pre * ROOT_HALF))
            put(ACT.at[l], rows, (pre * cumul).astype(bf16))
            put(GP.at[l], rows, (cumul + pre * (jnp.exp(-0.5 * pre * pre) * PHI_ZERO)).astype(bf16))

        if l == 1:
            w_pass(1, "down", 3)
            for copy in spills:
                copy.wait()
            weight_grad(1, "down", GF, ACT.at[1])
        w_pass(l, "down")
        w_done(l, "down")

        def feed_out(rows):
            return dot_nt(both(ACT.at[l], rows), W[l, :, 4 * HC + FC : 4 * HC + 2 * FC])

        if l == 0:
            rs_run(feed_out, {2: lambda: w_pass(1, "qkv", 1, 3)})
            w_pass(1, "qkv", 2, 3)

            @pl.loop(0, 2)
            def _(h):
                pl.when(h == 1)(lambda: w_pass(1, "qkv"))
                rs_wait(h)

                def layer_out(row, full):
                    X[1, row, :] = MID[0, row, :] + rs_sum(row) + vec[0, 5:6, :]
                    first_norm(1, row, full)

                by_chunk(h, layer_out)
                rs_end(h)
                ag_start(NF.at[1], h)

        else:

            @pl.loop(0, 4)
            def _(step):
                pre_back(1, pair(step % 2, step // 2))

            rs_run(lambda rows: dot_nt(both(GP.at[1], rows), W[1, :, 4 * HC : 4 * HC + FC]))
            weight_grad(1, "up", NF2.at[1], GP.at[1])
            g_upto(0)

        if l == 0:
            for g in range(len(groups)):
                w_sent(0, g)
            for copy in spills:
                copy.start()

    def last_out(row, full):
        STB[row, :] = (MID[1, row, :] + rs_sum(row) + vec[1, 5:6, :]).astype(bf16)

    def greet_pairs():
        for device in (sib, ypeer):
            pl.semaphore_signal(ack, inc=1, device_id=device, device_id_type=MESH)
        pl.semaphore_wait(ack, 2)

    for l in (1, 0):
        if l == 0:
            reload(3).wait()
            reload(2).wait()

        if l == 0:

            def feed_back(rows):
                PBUF[...] = dot_nt(pre_back(0, rows), W[1, :, 4 * HC : 4 * HC + FC])

            @pl.loop(0, 2)
            def _(h):
                ag_near(GF, h)
                feed_back(near_pair(h))
                rs_second(h)

            g_upto(9)


            @pl.loop(0, 2)
            def _(h):
                @pl.when(h == 1)
                def _():
                    rs_mid(0, PBUF[half:R, :])
                    g_upto(10)

                ag_far(GF, h)
                feed_back(far_pair(h))
                rs_first(h)

            rs_mid(1, PBUF[half:R, :])
            weight_grad(0, "down", GF, ACT.at[0])
            g_upto(11)
            vg_far(1)
            g_final(1, "down")
            g_upto(12)

        @pl.loop(0, 2)
        def _(h):
            rs_wait(h)

            def second_back(row, full):
                grad = GC[row, :] + norm_back(l, 3, rs_sum(row), MID[l, row, :], vec[l, 3:4, :])
                GC[row, :] = grad
                low = grad.astype(bf16)
                MF[full, :] = low
                vg[l, 2:3, :] += jnp.sum(low.astype(f32), axis=0, keepdims=True)

            by_chunk(h, second_back)
            rs_end(h)
            ag_start(MF, h)

            @pl.when(h == 0)
            def _():
                if l == 0:
                    weight_grad(0, "up", NF2.at[0], GP.at[0])
                g_upto(2 if l == 1 else 13)

        if l == 0:
            vg_tensor(1)
            g_final(1, "up")
            g_upto(14)
            reload(1).wait()
            reload(0).wait()
        if l == 1:
            g_upto(26)
            greet_pairs()
            rs_run(feed_out)
            g_upto(1)
        TR[...] = QKV[l, :, HC : 2 * HC].T
        DKA[...] = jnp.zeros_like(DKA)
        PBUF[...] = jnp.zeros_like(PBUF)

        @pl.loop(0, 4)
        def _(step):
            h = step % 2
            for place in (1, 2, 3):
                pl.when(step == place)(lambda: g_upto(place + (2 if l == 1 else 14)))
            pl.when(step < 2)(lambda: ag_near(MF, h))
            pl.when(step >= 2)(lambda: ag_far(MF, h))
            rows = pair(1 - step // 2, h)
            out_grads = dot_nn(both(MF, rows), W[1, :, 3 * HC : 4 * HC]).astype(bf16)
            queries = both(QKV.at[l, :, pl.ds(0, HC)], rows)
            keys = QKV[l, :, HC : 2 * HC]
            values = QKV[l, :, 2 * HC : 3 * HC]
            parts = []
            for head in range(heads):
                mask = head_mask(head)
                q_one = jnp.where(mask, queries, jnp.zeros_like(queries))
                do_one = jnp.where(mask, out_grads, jnp.zeros_like(out_grads))
                log_sum = jnp.concatenate([LSE[l, head : head + 1, rows[0]], LSE[l, head : head + 1, rows[1]]], axis=1)
                probs = jnp.exp2(dot_nt(keys, q_one) * (score_scale * LOG2E) - log_sum)
                prob_grad = dot_nt(values, do_one)
                value_part = dot_nn(probs.astype(bf16), do_one)
                for place in range(4):
                    PBUF[:, place * HC : (place + 1) * HC] += value_part[place * R : (place + 1) * R, :]
                row_dot = jnp.sum(probs * prob_grad, axis=0, keepdims=True)
                score_grad = (probs * (prob_grad - row_dot)).astype(bf16)
                DKA[...] += dot_nn(score_grad, q_one)
                parts.append(dot_nn(TR[head * HD : (head + 1) * HD, :], score_grad))
            query_low = (jnp.concatenate(parts, axis=0).T * score_scale).astype(bf16)
            put(DQKV.at[:, pl.ds(0, HC)], rows, query_low)

        g_upto(6 if l == 1 else 18)
        DQKV[:, HC : 2 * HC] = (DKA[...] * score_scale).astype(bf16)
        for place in range(4):
            DQKV[place * R : (place + 1) * R, 2 * HC : 3 * HC] = PBUF[:, place * HC : (place + 1) * HC].astype(bf16)
        weight_grad(l, "qkv", NF.at[l], DQKV)
        if l == 1:
            for g in range(len(groups)):
                w_sent(1, g)
            for at in (1, 2, 3):
                reload(at).start()

            @pl.loop(0, 2)
            def _(h):
                rs_wait(h)
                by_chunk(h, last_out)
                rs_end(h)

            mixed_copy = pltpu.make_async_copy(STB, mixed.at[0], loc.at[0, 6])
            mixed_copy.start()
            greet_pairs()
        g_upto(7 if l == 1 else 19)
        rs_run(lambda rows: dot_nt(both(DQKV, rows), W[1, :, 0 : 3 * HC]))
        if l == 1:
            reload(0).start()
        if l == 1:
            weight_grad(1, "out", MF, AT.at[1])
        vg[l, 7:8, 0:HC] = jnp.sum(DQKV[:, 0:HC].astype(f32), axis=0, keepdims=True)
        vg[l, 7:8, HC : 2 * HC] = jnp.sum(DQKV[:, 2 * HC : 3 * HC].astype(f32), axis=0, keepdims=True)
        g_upto(24 if l == 1 else 25)
        if l == 0:
            vg_end(1)

        @pl.loop(0, 2)
        def _(h):
            rs_wait(h)

            def first_back(row, full):
                grad = GC[row, :] + norm_back(l, 0, rs_sum(row), X[l, row, :], vec[l, 0:1, :])
                if l == 1:
                    low_grad(0, row, full, grad)
                else:
                    GC[row, :] = grad

            by_chunk(h, first_back)
            rs_end(h)
            if l == 1:
                ag_start(GF, h)

        vg_near(l)
        if l == 1:
            g_upto(8)
        else:
            weight_grad(0, "out", MF, AT.at[0])

    mixed_copy.wait()
    grad_copy = pltpu.make_async_copy(GC, tgrad.at[0], loc.at[0, 7])
    grad_copy.start()
    g_upto(20)
    vg_far(0)
    g_final(1, "qkv")
    g_final(1, "out")
    g_upto(21)
    vg_tensor(0)
    g_upto(22)
    g_upto(23)
    g_final(0, "down")
    g_final(0, "up")
    vg_end(0)
    g_final(0, "qkv")
    vs_copy = pltpu.make_async_copy(VS, vs_out, loc.at[0, 6])
    vs_copy.start()
    g_final(0, "out")
    grad_copy.wait()
    vs_copy.wait()
    for l in range(2):
        for g in range(len(groups)):
            g_sent(l, g)
        for name in spans:
            for copy in g_out(l, name):
                copy.wait()


def finish_kernel(S, *refs):
    sources, small, targets, smalls, stages, sems = refs[:8], refs[8], refs[9:17], refs[17:26], refs[26:34], refs[34]
    arrivals = [
        pltpu.make_async_copy(source, stage, sems.at[0, at]) for at, (source, stage) in enumerate(zip(sources, stages))
    ]
    copies = [
        pltpu.make_async_copy(stage, target, sems.at[1, at]) for at, (stage, target) in enumerate(zip(stages, targets))
    ]
    for arrival in arrivals:
        arrival.start()
    for arrival, copy in zip(arrivals, copies):
        arrival.wait()
        copy.start()
    for l in range(2):
        for place in range(8):
            smalls[place][l : l + 1, :] = small[l, place : place + 1, 0:S]
        for q in range(4):
            smalls[8][l : l + 1, q * S : (q + 1) * S] = small[l, 8 + q : 9 + q, 0:S]
    for copy in copies:
        copy.wait()


def shards(
    mesh_dp,
    tokens, clip_counts, cotangent, norm1_gain, norm1_shift, w_query, query_bias, w_key, w_value, value_bias, w_out,
    out_bias, norm2_gain, norm2_shift, w_up, up_bias, w_down, down_bias,
):
    layers, S, HC = w_query.shape
    FC = w_up.shape[2]
    _, R, D = tokens.shape
    B = 1
    while 4 * B * B <= mesh_dp:
        B *= 2
    A = mesh_dp // B
    LEN = 4 * R
    COLS = 4 * HC + 2 * FC
    dims = (A, B, S, R, D, HC, FC)
    parts = COLS // HC if A * B <= 16 else 4
    vm = pltpu.VMEM
    dma = pltpu.SemaphoreType.DMA
    any_spec = pl.BlockSpec(memory_space=pl.ANY)
    vmem_spec = pl.BlockSpec(memory_space=pltpu.VMEM)
    grad_small = jax.ShapeDtypeStruct((layers, S, HC), f32)
    grad_large = jax.ShapeDtypeStruct((layers, S, FC), f32)
    outs = pl.pallas_call(
        functools.partial(encoder_kernel, dims),
        out_shape=(
            jax.ShapeDtypeStruct((1, R, D), bf16),
            jax.ShapeDtypeStruct((1, R, D), f32),
            grad_small, grad_small, grad_small, grad_small, grad_large, grad_large,
            jax.ShapeDtypeStruct((layers, 16, 128), f32),
            jax.ShapeDtypeStruct((D, COLS), bf16),
        ),
        in_specs=[any_spec, any_spec, pl.BlockSpec(memory_space=pltpu.SMEM)] + [any_spec] * 6 + [vmem_spec] * 9,
        out_specs=tuple([any_spec] * 10),
        scratch_shapes=[
            vm((2, D, COLS), bf16),
            vm((2, LEN, D), bf16),
            vm((2, LEN, 3 * HC), bf16),
            vm((2, LEN, HC), bf16),
            vm((2, 8, LEN), f32),
            vm((2, R, D), f32),
            vm((2, R, D), f32),
            vm((2, LEN, D), bf16),
            vm((2, LEN, FC), bf16),
            vm((2, LEN, FC), bf16),
            vm((LEN, D), bf16),
            vm((LEN, D), bf16),
            vm((LEN, 3 * HC), bf16),
            vm((R, D), f32),
            vm((max(B - 1, 1), A, S, COLS), bf16),
            vm((max(A - 1, 1), S, COLS), bf16),
            vm((R, D), bf16), vm((R, D), bf16), vm((R, D), bf16),
            vm((R, D), bf16), vm((R, D), bf16), vm((R, D), bf16),
            vm((R, D), f32), vm((R, D), f32),
            vm((2, S, COLS), f32),
            vm((HC, LEN), bf16),
            vm((LEN, HC), f32),
            vm((R, D), bf16),
            vm((A * B, 24, 128), f32),
            vm((2, 8, D), f32), vm((2, 8, D), f32),
            vm((2, max(B - 1, 1), 8, D), f32),
            vm((2, 8, D), f32),
            vm((2, max(A - 1, 1), 8, D), f32),
            vm((2, 8, D), f32),
            vm((2, 3, 8, D), f32),
            vm((2, 16, 128), f32),
            vm((16, D), f32),
            dma((2, 10)),
            dma((2, 2, 3)), dma((2, 2, 3)), dma((2, 3)), dma((2, 3)),
            dma((2 * parts, 2, A)), dma((2 * parts, 2, A)), dma((2 * parts, A, B)), dma((2 * parts, A, B)),
            dma((2, parts, B, A)), dma((2, parts, B, A)), dma((2, parts, A)), dma((2, parts, A)),
            dma((A,)), dma((A,)), dma((A, B)), dma((A, B)),
            dma((2, B)), dma((2, B)), dma((2, A)), dma((2, A)), dma((2, 4)), dma((2, 4)),
            pltpu.SemaphoreType.REGULAR((parts,)), pltpu.SemaphoreType.REGULAR((parts,)), pltpu.SemaphoreType.REGULAR,
        ],
        compiler_params=pltpu.CompilerParams(
            collective_id=0, has_side_effects=True, vmem_limit_bytes=64 * 2**20 - 2**17
        ),
        name="encoder",
    )(tokens, cotangent, clip_counts, w_query, w_key, w_value, w_out, w_up, w_down, norm1_gain, norm1_shift,
      out_bias, norm2_gain, norm2_shift, down_bias, query_bias, value_bias, up_bias)

    small = jax.ShapeDtypeStruct((layers, S), f32)
    large_types = tuple(jax.ShapeDtypeStruct(member.shape, member.dtype) for member in outs[:8])
    (mixed, tokens_grad, gq, gk, gv, go, gu, gd, g_gain_one, g_shift_one, g_out, g_gain_two, g_shift_two, g_down, g_query,
     g_value, g_up) = pl.pallas_call(
        functools.partial(finish_kernel, S),
        out_shape=large_types + (small,) * 8 + (jax.ShapeDtypeStruct((layers, 4 * S), f32),),
        in_specs=[any_spec] * 8 + [vmem_spec],
        out_specs=tuple([any_spec] * 8 + [vmem_spec] * 9),
        scratch_shapes=[vm(member.shape, member.dtype) for member in outs[:8]] + [dma((2, 8))],
        compiler_params=pltpu.CompilerParams(vmem_limit_bytes=64 * 2**20 - 2**17),
        name="finish",
    )(*outs[:9])
    return (
        mixed, tokens_grad, g_gain_one, g_shift_one, gq, g_query, gk, gv, g_value, go, g_out, g_gain_two, g_shift_two, gu,
        g_up, gd, g_down,
    )


def solution(mesh):
    rows = P("dp", "tensor", None)
    vector = P(None, "dp")
    matrix = P(None, "dp", "tensor")
    return jax.shard_map(
        functools.partial(shards, mesh.shape["dp"]),
        mesh=mesh,
        in_specs=(
            rows, P("dp"), rows, vector, vector, matrix, vector, matrix, matrix, vector, matrix, vector, vector, vector,
            matrix, vector, matrix, vector,
        ),
        out_specs=(
            rows, rows, vector, vector, matrix, vector, matrix, matrix, vector, matrix, vector, vector, vector, matrix,
            vector, matrix, vector,
        ),
        check_vma=False,
    )
```
